256 devices in a mesh: row: 4 (over x), col: 4 (over y), depth: 16 (over z, core).
Axes of the slice: x: 4, y: 4, z: 8, core: 2. Of those that a mesh axis runs over, the one named last changes fastest.
Arguments:
- pair: bfloat16 [640, 640, 128], P('row', 'col'), may hold values from -6 to 6
- in_gain: float32 [2, 128], replicated, may hold values from 0.25 to 1.75
- in_bias: float32 [2, 128], replicated, may hold values from -3 to 3
- proj_weight: bfloat16 [2, 128, 512], replicated, may hold values from -0.5 to 0.5
- gate_weight: bfloat16 [2, 128, 128], replicated, may hold values from -0.5 to 0.5
- out_gain: float32 [2, 128], replicated, may hold values from 0.25 to 1.75
- out_bias: float32 [2, 128], replicated, may hold values from -3 to 3
- out_weight: bfloat16 [2, 128, 128], replicated, may hold values from -0.5 to 0.5
Outputs:
- updated: bfloat16 [640, 640, 128], P('row', 'col')
The draws below stay inside these ranges and needn't reach their ends.
All inputs are finite; a program needn't handle non-finite values.
Results may differ from the reference program's by a relative error of at most 0.015.
Values may be sent and summed in bfloat16 or wider, within the bound.
No kernel may reach another device: no remote copies, remote signals or barrier semaphores. Data moves between devices by JAX's collectives and lax.ppermute only.
A program may use at most 128 MiB of HBM per device.

```python
import jax
import jax.numpy as jnp
from jax import lax

C = 128
N = 640
N_ROW = 4
N_COL = 4


def block_scale(rng, shape, pieces, smallest, top_value):
    level, own = 1.0, jax.random.fold_in(rng, 6)
    for position, shards_of in pieces:
        heights = jnp.exp(jax.random.uniform(jax.random.fold_in(own, position), (shards_of,), jnp.float32, smallest / len(pieces), top_value / len(pieces)))
        level = level * jnp.repeat(heights, shape[position] // shards_of).reshape([-1 if axis == position else 1 for axis in range(len(shape))])
    return level


def noise(own_key, dims, deviation, reach, cuts=(), held_as=jnp.bfloat16):
    entries = jax.random.normal(own_key, dims, jnp.float32) * deviation
    if len(cuts) > 0:
        entries = block_scale(own_key, dims, cuts, -0.22, 0.18) * entries
    return jnp.clip(entries, min=-reach, max=reach).astype(held_as)


def setup_inputs(seed: int = 0) -> dict:
    splits = jax.random.split(jax.random.key(seed), 9)
    pair = noise(splits[0], (N, N, C), 1.0, 6.0, ((0, 4), (1, 4)))
    in_gain = jnp.clip(1.0 + 0.15 * jax.random.normal(splits[1], (2, C), jnp.float32), 0.25, 1.75)
    in_bias = noise(splits[2], (2, C), 0.5, 3.0, (), jnp.float32)
    proj_weight = noise(splits[3], (2, C, 4 * C), C ** -0.5, 0.5)
    gate_weight = noise(splits[4], (2, C, C), C ** -0.5, 0.5)
    out_gain = jnp.clip(1.0 + 0.15 * jax.random.normal(splits[5], (2, C), jnp.float32), 0.25, 1.75)
    out_bias = noise(splits[6], (2, C), 0.5, 3.0, (), jnp.float32)
    out_weight = noise(splits[7], (2, C, C), C ** -0.5, 0.5)
    return {"pair": pair, "in_gain": in_gain, "in_bias": in_bias, "proj_weight": proj_weight, "gate_weight": gate_weight, "out_gain": out_gain, "out_bias": out_bias, "out_weight": out_weight}


def normalize(values, gain, bias):
    values = values.astype(jnp.float32)
    mean = lax.optimization_barrier(jnp.mean(values, axis=-1, keepdims=True))
    centred = values - mean
    spread = lax.optimization_barrier(jnp.mean(centred * centred, axis=-1, keepdims=True))
    return centred * lax.rsqrt(spread + 1e-05) * gain + bias

def gated(normed, weight):
    width = weight.shape[1] // 2
    hidden = jnp.dot(normed, weight, preferred_element_type=jnp.float32)
    return (jax.nn.sigmoid(hidden[..., width:]) * hidden[..., :width]).astype(jnp.bfloat16)

def blocked_outgoing(left, right, blocks):
    length = left.shape[1]
    size = length // blocks
    total = jnp.zeros((left.shape[0], right.shape[0], left.shape[2]), jnp.float32)
    for g in range(blocks):
        piece = jnp.einsum('ikc,jkc->ijc', left[:, g * size:(g + 1) * size], right[:, g * size:(g + 1) * size], precision=lax.Precision.HIGHEST)
        total = total + piece.astype(jnp.bfloat16).astype(jnp.float32)
    return total

def blocked_incoming(left, right, blocks):
    length = left.shape[0]
    size = length // blocks
    total = jnp.zeros((left.shape[1], right.shape[1], left.shape[2]), jnp.float32)
    for g in range(blocks):
        piece = jnp.einsum('kic,kjc->ijc', left[g * size:(g + 1) * size], right[g * size:(g + 1) * size], precision=lax.Precision.HIGHEST)
        total = total + piece.astype(jnp.bfloat16).astype(jnp.float32)
    return total

def triangle(field, which, in_gain, in_bias, proj_weight, gate_weight, out_gain, out_bias, out_weight, incoming):
    chans = field.shape[2]
    normed = normalize(field, in_gain[which], in_bias[which]).astype(jnp.bfloat16)
    left = gated(normed, proj_weight[which][:, :2 * chans]).astype(jnp.float32)
    right = gated(normed, proj_weight[which][:, 2 * chans:]).astype(jnp.float32)
    gate = jax.nn.sigmoid(jnp.dot(normed, gate_weight[which], preferred_element_type=jnp.float32))
    if incoming:
        tri = blocked_incoming(left, right, N_ROW)
    else:
        tri = blocked_outgoing(left, right, N_COL)
    upd = normalize(tri, out_gain[which], out_bias[which]).astype(jnp.bfloat16)
    result = field.astype(jnp.float32) + gate * jnp.dot(upd, out_weight[which], preferred_element_type=jnp.float32)
    return result.astype(jnp.bfloat16)

def reference(pair, in_gain, in_bias, proj_weight, gate_weight, out_gain, out_bias, out_weight):
    middle = triangle(pair, 0, in_gain, in_bias, proj_weight, gate_weight, out_gain, out_bias, out_weight, False)
    return triangle(middle, 1, in_gain, in_bias, proj_weight, gate_weight, out_gain, out_bias, out_weight, True)
```

```python
import functools

import jax
import jax.numpy as jnp
from jax import lax
from jax.experimental import pallas as pl
from jax.experimental.pallas import tpu as pltpu
from jax.sharding import PartitionSpec as P

F32 = jnp.float32
BF16 = jnp.bfloat16
VMEM_LIMIT = 60 * 1024 * 1024
NT = (((1,), (1,)), ((), ()))


def norm_rows(values, gain, bias):
    mean = jnp.mean(values, axis=-1, keepdims=True)
    centred = values - mean
    spread = jnp.mean(centred * centred, axis=-1, keepdims=True)
    return centred * lax.rsqrt(spread + 1e-05) * gain + bias


def norm_chans(values, gain, bias):
    mean = jnp.mean(values, axis=0, keepdims=True)
    centred = values - mean
    spread = jnp.mean(centred * centred, axis=0, keepdims=True)
    return centred * lax.rsqrt(spread + 1e-05) * gain + bias


def widen_rows(rows):
    return jnp.concatenate([rows, jnp.zeros((256 - rows.shape[0], rows.shape[1]), rows.dtype)], axis=0)


def fold(tail):
    total = tail[:16]
    for m in range(1, 4):
        total = total + pltpu.roll(tail[16 * m : 16 * m + 16], 32 * m, 1)
    return total


def unfold(packed):
    parts = [packed] + [pltpu.roll(packed, 128 - 32 * m, 1) for m in range(1, 4)]
    tail = jnp.concatenate(parts, axis=0)
    lane = lax.broadcasted_iota(jnp.int32, tail.shape, 1)
    return jnp.where(lane < 32, tail, 0.0)


def pack(chans):
    return jnp.concatenate([chans[:, :128], fold(chans[:, 128:])], axis=0).astype(BF16)


def unpack(block):
    wide = block.astype(F32)
    return jnp.concatenate([wide[:64], unfold(wide[64:])], axis=1)


def gated_chans(weight_t, normed):
    hidden = lax.dot_general(weight_t, normed, NT, preferred_element_type=F32)
    n = weight_t.shape[0] // 2
    return jax.nn.sigmoid(hidden[n:]) * hidden[:n]


def share_kernel(x_ref, gain_ref, bias_ref, weight_ref, out_ref):
    rows = x_ref.shape[0]
    for r in range(rows):
        normed = norm_rows(x_ref[r].astype(F32), gain_ref[...], bias_ref[...]).astype(BF16)
        out_ref[r] = pack(gated_chans(weight_ref[...], widen_rows(normed)))


def tile_kernel(steps, per, x_ref, gain_ref, bias_ref, weight_ref, out_ref, main, tail):
    step = pl.program_id(0)
    for r in range(per):
        normed = norm_rows(x_ref[r].astype(F32), gain_ref[...], bias_ref[...]).astype(BF16)
        values = gated_chans(weight_ref[...], widen_rows(normed))
        row = step * per + r
        main[pl.ds(row, 64, stride=160), :] = values[:, :128]
        tail[pl.ds(row, 64, stride=160), :] = values[:, 128:]

    @pl.when(step == steps - 1)
    def _():
        def put(c, carry):
            at = pl.ds(pl.multiple_of(c * 160, 8), 160)
            out_ref[c] = jnp.concatenate([main[at, :], tail[at, :]], axis=1).astype(BF16)
            return carry

        lax.fori_loop(0, 64, put, 0)


def contract_kernel(big_is_packed, *refs):
    if big_is_packed:
        swap_ref, big_ref, small_ref, out_ref, main, tail, bmain, btail = refs
        half = swap_ref[0]

        def spread_big(b, carry):
            z, rest = b // 20, lax.rem(b, 20)
            o, j = rest // 10, lax.rem(rest, 10)
            row = z * 20 + jnp.where(half == 0, o, 1 - o) * 10 + j
            wide = unpack(big_ref[b])
            bmain[pl.ds(row, 64, stride=160), :] = wide[:, :128]
            btail[pl.ds(row, 64, stride=160), :] = wide[:, 128:]
            return carry

        lax.fori_loop(0, 160, spread_big, 0, unroll=4)
    else:
        big_ref, small_ref, out_ref, main, tail = refs

    def spread(b, carry):
        wide = unpack(small_ref[b])
        main[pl.ds(b, 64, stride=80), :] = wide[:, :128]
        tail[pl.ds(b, 64, stride=80), :] = wide[:, 128:]
        return carry

    lax.fori_loop(0, 80, spread, 0, unroll=4)

    def multiply(c, carry):
        at = pl.ds(pl.multiple_of(c * 80, 8), 80)
        small = jnp.concatenate([main[at, :], tail[at, :]], axis=1).astype(BF16)
        if big_is_packed:
            bat = pl.ds(pl.multiple_of(c * 160, 8), 160)
            big = jnp.concatenate([bmain[bat, :], btail[bat, :]], axis=1).astype(BF16)
        else:
            big = big_ref[c]
        product = lax.dot_general(small, big, NT, preferred_element_type=F32)
        main[at, :] = product[:, :128]
        tail[at, :] = jnp.concatenate([product[:, 128:], jnp.zeros((80, 96), F32)], axis=1)
        return carry

    lax.fori_loop(0, 64, multiply, 0, unroll=4)

    def collect(b, carry):
        out_ref[b] = jnp.concatenate(
            [main[pl.ds(b, 64, stride=80), :], fold(tail[pl.ds(b, 64, stride=80), :])], axis=0
        ).astype(BF16)
        return carry

    lax.fori_loop(0, 80, collect, 0, unroll=4)


def middle_kernel(
    own_ref, other_ref, x_ref, gain0_ref, bias0_ref, gatew_ref, ogain_ref, obias_ref, outw_ref,
    gain1_ref, bias1_ref, projw_ref, mid_ref, keep_ref, send_ref,
):
    lane = lax.broadcasted_iota(jnp.int32, (128, 256), 1)
    eye = (lax.broadcasted_iota(jnp.int32, (128, 128), 0) == lax.broadcasted_iota(jnp.int32, (128, 128), 1))
    eye = eye.astype(F32).astype(BF16)
    for s in range(own_ref.shape[0]):
        tri = jnp.concatenate([unpack(own_ref[s]), unpack(other_ref[s])], axis=0)
        upd = norm_chans(tri, ogain_ref[...], obias_ref[...]).astype(BF16)
        turned = jnp.dot(outw_ref[...], upd, preferred_element_type=F32)
        x = x_ref[s]
        normed = norm_rows(x.astype(F32), gain0_ref[...], bias0_ref[...]).astype(BF16)
        gate = jax.nn.sigmoid(
            lax.dot_general(gatew_ref[...], widen_rows(normed), NT, preferred_element_type=F32)
        )
        field = lax.dot_general(eye, widen_rows(x), NT, preferred_element_type=F32)
        middle = (field + gate * turned).astype(BF16)
        wide = middle.astype(F32)
        mid_ref[s] = jnp.transpose(wide)[:160].astype(BF16)
        normed1 = norm_chans(wide, gain1_ref[...], bias1_ref[...]).astype(BF16)
        hidden = jnp.dot(projw_ref[...], normed1, preferred_element_type=F32)
        for side in range(2):
            h = hidden[256 * side : 256 * side + 256]
            value = jnp.where(lane < 160, jax.nn.sigmoid(h[128:]) * h[:128], 0.0)
            keep_ref[side, s] = pack(value[:64])
            send_ref[side, s] = pack(value[64:])


def last_kernel(
    own_ref, other_ref, x_ref, gain_ref, bias_ref, gatew_ref, ogain_ref, obias_ref, outw_ref, out_ref
):
    for s in range(own_ref.shape[0]):
        tri = jnp.concatenate([unpack(own_ref[s]), unpack(other_ref[s])], axis=0)
        upd = norm_chans(tri, ogain_ref[...], obias_ref[...])
        upd = jnp.transpose(upd)[:160].astype(BF16)
        x = x_ref[s].astype(F32)
        normed = norm_rows(x, gain_ref[...], bias_ref[...]).astype(BF16)
        gate = jax.nn.sigmoid(jnp.dot(normed, gatew_ref[...], preferred_element_type=F32))
        turned = jnp.dot(upd, outw_ref[...], preferred_element_type=F32)
        out_ref[s] = (x + gate * turned).astype(BF16)


def params():
    return pltpu.CompilerParams(vmem_limit_bytes=VMEM_LIMIT)


def whole(shape):
    zeros = (0,) * len(shape)
    return pl.BlockSpec(shape, lambda *_: zeros)


def share_call(x, gain, bias, weight_t):
    return pl.pallas_call(
        share_kernel,
        grid=(4,),
        in_specs=[
            pl.BlockSpec((5, 160, 128), lambda b: (b, 0, 0)),
            whole((1, 128)), whole((1, 128)), whole((128, 128)),
        ],
        out_specs=pl.BlockSpec((5, 80, 128), lambda b: (b, 0, 0)),
        out_shape=jax.ShapeDtypeStruct((20, 80, 128), BF16),
        compiler_params=params(),
        name="share",
    )(x, gain, bias, weight_t)


def tile_call(x, gain, bias, weight_t):
    per = 8
    steps = 160 // per
    return pl.pallas_call(
        functools.partial(tile_kernel, steps, per),
        grid=(steps,),
        in_specs=[
            pl.BlockSpec((per, 160, 128), lambda b: (b, 0, 0)),
            whole((1, 128)), whole((1, 128)), whole((128, 128)),
        ],
        out_specs=whole((64, 160, 256)),
        out_shape=jax.ShapeDtypeStruct((64, 160, 256), BF16),
        scratch_shapes=[pltpu.VMEM((64 * 160, 128), F32)] * 2,
        compiler_params=params(),
        cost_estimate=pl.CostEstimate(flops=2 * 25600 * 128 * 128, bytes_accessed=30 * 2**20, transcendentals=25600 * 64),
        name="tile",
    )(x, gain, bias, weight_t)


def contract_call(big, small, half=None):
    packed = half is not None
    scratch = [pltpu.VMEM((64 * 80, 128), F32)] * 2
    args = [big, small]
    specs = [whole(big.shape), whole(small.shape)]
    if packed:
        scratch = scratch + [pltpu.VMEM((64 * 160, 128), F32)] * 2
        args = [half] + args
        specs = [pl.BlockSpec(memory_space=pltpu.SMEM)] + specs
    return pl.pallas_call(
        functools.partial(contract_kernel, packed),
        grid=(1,),
        in_specs=specs,
        out_specs=whole((80, 80, 128)),
        out_shape=jax.ShapeDtypeStruct((80, 80, 128), BF16),
        scratch_shapes=scratch,
        compiler_params=params(),
        name="contract",
    )(*args)


def middle_call(own, other, x, *rest):
    per, steps = 5, 2
    block = pl.BlockSpec((per, 80, 128), lambda b: (b, 0, 0))
    rows = pl.BlockSpec((per, 160, 128), lambda b: (b, 0, 0))
    pair = pl.BlockSpec((2, per, 80, 128), lambda b: (0, b, 0, 0))
    return pl.pallas_call(
        middle_kernel,
        grid=(steps,),
        in_specs=[block, block, rows] + [whole(r.shape) for r in rest],
        out_specs=[rows, pair, pair],
        out_shape=[
            jax.ShapeDtypeStruct((10, 160, 128), BF16),
            jax.ShapeDtypeStruct((2, 10, 80, 128), BF16),
            jax.ShapeDtypeStruct((2, 10, 80, 128), BF16),
        ],
        compiler_params=params(),
        name="middle",
    )(own, other, x, *rest)


def last_call(own, other, x, *rest):
    per, steps = 5, 2
    block = pl.BlockSpec((per, 80, 128), lambda b: (b, 0, 0))
    rows = pl.BlockSpec((per, 160, 128), lambda b: (b, 0, 0))
    return pl.pallas_call(
        last_kernel,
        grid=(steps,),
        in_specs=[block, block, rows] + [whole(r.shape) for r in rest],
        out_specs=rows,
        out_shape=jax.ShapeDtypeStruct((10, 160, 128), BF16),
        compiler_params=params(),
        name="last",
    )(own, other, x, *rest)


def on_device(pair, in_gain, in_bias, proj_weight, gate_weight, out_gain, out_bias, out_weight):
    layer = lax.axis_index("depth")
    z, half = layer // 2, layer % 2
    swap = [(d, d ^ 1) for d in range(16)]
    same_core = [list(range(0, 16, 2)), list(range(1, 16, 2))]

    def local(values, axis):
        return jnp.where(half == 0, values, jnp.roll(values, 64, axis))

    def mine(values):
        return lax.dynamic_slice_in_dim(values, 64 * half, 64, 1)

    p0 = proj_weight[0]
    left_w = jnp.concatenate([mine(p0[:, :128]), mine(p0[:, 128:256])], axis=1).T
    right_w = jnp.concatenate([mine(p0[:, 256:384]), mine(p0[:, 384:])], axis=1).T
    gain0, bias0 = in_gain[0:1], in_bias[0:1]
    share = lax.dynamic_slice_in_dim(pair, 20 * z, 20, 0).reshape(2, 10, 160, 128)
    share = jnp.where(half == 0, share, share[::-1]).reshape(20, 160, 128)
    right = share_call(share, gain0, bias0, right_w)
    right_all = lax.all_gather(right, "row", axis=0, tiled=True)
    left = tile_call(pair, gain0, bias0, left_w)
    products = contract_call(left, right_all)
    sums = lax.psum_scatter(products, "col", scatter_dimension=0, tiled=True)
    other = lax.ppermute(sums[10:], "depth", swap)

    columns = lax.dynamic_slice_in_dim(pair, 10 * layer, 10, 1).transpose(1, 0, 2)
    p1 = proj_weight[1]
    proj1 = jnp.concatenate([local(p1[:, 128 * s : 128 * s + 128], 1) for s in range(4)], axis=1).T
    middle, keep, send = middle_call(
        sums[:10], other, columns, gain0, bias0, gate_weight[0].T,
        local(out_gain[0], 0)[:, None], local(out_bias[0], 0)[:, None], local(out_weight[0], 0).T,
        in_gain[1][:, None], in_bias[1][:, None], proj1,
    )
    got = lax.ppermute(send, "depth", swap)
    left1 = jnp.concatenate([keep[0], got[0]], axis=0)
    right1 = jnp.concatenate([keep[1], got[1]], axis=0)
    right1_all = lax.all_gather(right1, "depth", axis=0, tiled=True, axis_index_groups=same_core)
    left1_all = lax.all_gather(left1, "col", axis=0, tiled=True)
    spread = lax.all_to_all(middle.reshape(10, 16, 10, 128), "depth", 1, 0, tiled=False)
    rows = spread.reshape(160, 10, 128).transpose(1, 0, 2)
    products1 = contract_call(right1_all, left1_all, half.astype(jnp.int32).reshape(1))
    sums1 = lax.psum_scatter(products1, "row", scatter_dimension=0, tiled=True)
    other1 = lax.ppermute(sums1[10:], "depth", swap)
    result = last_call(
        sums1[:10], other1, rows, in_gain[1:2], in_bias[1:2], gate_weight[1],
        local(out_gain[1], 0)[:, None], local(out_bias[1], 0)[:, None], local(out_weight[1], 0),
    )
    return lax.all_gather(result, "depth", axis=0, tiled=True)


def solution(mesh):
    placed = (P("row", "col", None), P(), P(), P(), P(), P(), P(), P())
    return jax.shard_map(
        on_device, mesh=mesh, in_specs=placed, out_specs=P("row", "col", None), check_vma=False
    )
```

```python
import functools

import jax
import jax.numpy as jnp
from jax import lax
from jax.experimental import pallas as pl
from jax.experimental.pallas import tpu as pltpu
from jax.sharding import PartitionSpec as P

F32 = jnp.float32
BF16 = jnp.bfloat16
VMEM_LIMIT = 60 * 1024 * 1024
NT = (((1,), (1,)), ((), ()))


def norm_rows(values, gain, bias):
    mean = jnp.mean(values, axis=-1, keepdims=True)
    centred = values - mean
    spread = jnp.mean(centred * centred, axis=-1, keepdims=True)
    return centred * lax.rsqrt(spread + 1e-05) * gain + bias


def norm_chans(values, gain, bias):
    mean = jnp.mean(values, axis=0, keepdims=True)
    centred = values - mean
    spread = jnp.mean(centred * centred, axis=0, keepdims=True)
    return centred * lax.rsqrt(spread + 1e-05) * gain + bias


def widen_rows(rows):
    return jnp.concatenate([rows, jnp.zeros((256 - rows.shape[0], rows.shape[1]), rows.dtype)], axis=0)


def fold(tail):
    total = tail[:16]
    for m in range(1, 4):
        total = total + pltpu.roll(tail[16 * m : 16 * m + 16], 32 * m, 1)
    return total


def unfold(packed):
    parts = [packed] + [pltpu.roll(packed, 128 - 32 * m, 1) for m in range(1, 4)]
    tail = jnp.concatenate(parts, axis=0)
    lane = lax.broadcasted_iota(jnp.int32, tail.shape, 1)
    return jnp.where(lane < 32, tail, 0.0)


def pack(chans):
    return jnp.concatenate([chans[:, :128], fold(chans[:, 128:])], axis=0).astype(BF16)


def unpack(block):
    wide = block.astype(F32)
    return jnp.concatenate([wide[:64], unfold(wide[64:])], axis=1)


def gated_chans(weight_t, normed):
    hidden = lax.dot_general(weight_t, normed, NT, preferred_element_type=F32)
    n = weight_t.shape[0] // 2
    return jax.nn.sigmoid(hidden[n:]) * hidden[:n]


def swap_major(values):
    return jnp.swapaxes(values, 0, 1)


def pick_weight(weight_ref, half, first):
    both = []
    for start in (first, first + 128):
        pane = weight_ref[0, :, start : start + 128].astype(F32)
        both.append(jnp.where(half == 0, pane[:, :64], pane[:, 64:]))
    return jnp.transpose(jnp.concatenate(both, axis=1)).astype(BF16)


def share_kernel(info_ref, x_ref, gain_ref, bias_ref, weight_ref, out_ref, weight):
    @pl.when(pl.program_id(0) == 0)
    def _():
        weight[...] = pick_weight(weight_ref, info_ref[1], 256)

    for r in range(x_ref.shape[0]):
        normed = norm_rows(x_ref[r].astype(F32), gain_ref[0:1], bias_ref[0:1]).astype(BF16)
        out_ref[r] = pack(gated_chans(weight[...], widen_rows(normed)))


def tile_kernel(info_ref, x_ref, gain_ref, bias_ref, weight_ref, out_ref, weight):
    @pl.when(pl.program_id(0) == 0)
    def _():
        weight[...] = pick_weight(weight_ref, info_ref[1], 0)

    rows = []
    for r in range(x_ref.shape[0]):
        normed = norm_rows(x_ref[r].astype(F32), gain_ref[0:1], bias_ref[0:1]).astype(BF16)
        rows.append(gated_chans(weight[...], widen_rows(normed)).astype(BF16))
    for side in range(2):
        at = slice(128 * side, 128 * side + 128)
        out_ref[:, :, at] = swap_major(jnp.stack([row[:, at] for row in rows]))


def spread_blocks(blocks, main, tail, groups, mask):
    def step(g, carry):
        at = pl.ds(pl.multiple_of(g * 16, 16), 16)
        x = blocks[at]
        main[:, at, :] = swap_major(x[:, :64])
        folded = swap_major(x[:, 64:]).astype(F32).reshape(256, 128)
        lane = lax.broadcasted_iota(jnp.int32, (256, 128), 1)
        for m in range(4):
            part = folded if m == 0 else pltpu.roll(folded, 128 - 32 * m, 1)
            if mask:
                part = jnp.where(lane < 32, part, 0.0)
            tail[16 * m : 16 * m + 16, at, :] = part.astype(BF16).reshape(16, 16, 128)
        return carry

    lax.fori_loop(0, groups, step, 0)


def contract_kernel(n_big, n_small, info_ref, *refs):
    z, half, shift = info_ref[0], info_ref[1], info_ref[2]
    big_refs, refs = refs[:n_big], refs[n_big:]
    small_refs, refs = refs[:n_small], refs[n_small:]
    out_refs, refs = refs[:8], refs[8:]
    sblk, smain, stail, omain, otail = refs[:5]
    pieces = n_small // 4
    for t in range(4):
        spot = lax.rem(t + shift, 4) * 20
        for s in range(pieces):
            ref = small_refs[t * pieces + s]
            n = ref.shape[1]
            for o in range(2):
                sblk[pl.ds(spot + 10 * o + n * s, n)] = ref[o]
    spread_blocks(sblk, smain, stail, 5, True)
    if n_big > 1:
        bblk, bmain, btail = refs[5:]
        for p in range(8):
            spot = lax.rem(z + p, 8) * 20
            for o in range(2):
                sh = half if o == 0 else 1 - half
                piece = big_refs[p][o] if p < 4 else big_refs[4 + o][...] if p == 4 else big_refs[p + 1][o]
                bblk[pl.ds(spot + 10 * sh, 10)] = piece
        spread_blocks(bblk, bmain, btail, 10, False)

    def multiply(rho, carry):
        ends = []
        for m in range(4):
            c = 16 * m + rho
            small = jnp.concatenate([smain[c], stail[c]], axis=1)
            big = big_refs[0][c] if n_big == 1 else jnp.concatenate([bmain[c], btail[c]], axis=1)
            product = lax.dot_general(small, big, NT, preferred_element_type=F32)
            omain[c] = product[:, :128].astype(BF16)
            ends.append(product[:, 128:])
        otail[rho] = jnp.concatenate(ends, axis=1).astype(BF16)
        return carry

    lax.fori_loop(0, 16, multiply, 0, unroll=4)
    for g in range(5):
        at = slice(16 * g, 16 * g + 16)
        main = swap_major(omain[:, at, :])
        tail = swap_major(otail[:, at, :])
        for r in range(16):
            b = 16 * g + r
            out = out_refs[b // 10]
            out[b % 10, :64] = main[r]
            out[b % 10, 64:] = tail[r]


def turn(values):
    return jnp.transpose(values.astype(F32))


def prep_kernel(
    info_ref, x_ref, gain_ref, bias_ref, projw_ref, gatew_ref, ogain_ref, obias_ref, outw_ref,
    gate_ref, field_ref, proj_ref, out0_ref, out1_ref, scales_ref,
):
    half = info_ref[1]

    def local(values):
        return jnp.where(half == 0, values, jnp.concatenate([values[64:], values[:64]], axis=0))

    def column(row):
        return jnp.transpose(jnp.broadcast_to(row, (128, 128)))

    for s in range(4):
        proj_ref[128 * s : 128 * s + 128] = local(turn(projw_ref[1, :, 128 * s : 128 * s + 128])).astype(BF16)
    rolled = local(outw_ref[0].astype(F32))
    out0_ref[...] = jnp.transpose(rolled).astype(BF16)
    out1_ref[...] = local(outw_ref[1].astype(F32)).astype(BF16)
    for n, row in enumerate((ogain_ref[0:1], obias_ref[0:1], ogain_ref[1:2], obias_ref[1:2])):
        scales_ref[n] = local(column(row))
    scales_ref[4] = column(gain_ref[1:2])
    scales_ref[5] = column(bias_ref[1:2])
    gate_w = turn(gatew_ref[0]).astype(BF16)
    eye = lax.broadcasted_iota(jnp.int32, (128, 128), 0) == lax.broadcasted_iota(jnp.int32, (128, 128), 1)
    eye = eye.astype(F32).astype(BF16)
    for s in range(x_ref.shape[0]):
        x = x_ref[s]
        normed = norm_rows(x.astype(F32), gain_ref[0:1], bias_ref[0:1]).astype(BF16)
        gate_ref[s] = jax.nn.sigmoid(
            lax.dot_general(gate_w, widen_rows(normed), NT, preferred_element_type=F32)
        )
        field = lax.dot_general(eye, widen_rows(x), NT, preferred_element_type=F32)
        field_ref[s] = field.astype(BF16)


def wide(scale):
    return jnp.concatenate([scale, scale], axis=1)


def middle_kernel(
    own0_ref, own1_ref, own2_ref, other_ref, gate_ref, field_ref, proj_ref, outw_ref, scales_ref,
    mid_ref, keepl_ref, keepr_ref, sendl_ref, sendr_ref,
):
    lane = lax.broadcasted_iota(jnp.int32, (128, 256), 1)
    for s in range(gate_ref.shape[0]):
        own = own0_ref[s].astype(F32) + own1_ref[s].astype(F32) + own2_ref[s].astype(F32)
        tri = jnp.concatenate([unpack(own), unpack(other_ref[s])], axis=0)
        upd = norm_chans(tri, wide(scales_ref[0]), wide(scales_ref[1])).astype(BF16)
        turned = jnp.dot(outw_ref[...], upd, preferred_element_type=F32)
        middle = (field_ref[s].astype(F32) + gate_ref[s] * turned).astype(BF16).astype(F32)
        mid_ref[s] = jnp.transpose(middle)[:160].astype(BF16)
        normed = norm_chans(middle, wide(scales_ref[4]), wide(scales_ref[5])).astype(BF16)
        hidden = jnp.dot(proj_ref[...], normed, preferred_element_type=F32)
        for side, (keep_ref, send_ref) in enumerate(((keepl_ref, sendl_ref), (keepr_ref, sendr_ref))):
            h = hidden[256 * side : 256 * side + 256]
            value = jnp.where(lane < 160, jax.nn.sigmoid(h[128:]) * h[:128], 0.0)
            keep_ref[s] = pack(value[:64])
            send_ref[s] = pack(value[64:])


def gate_kernel(x_ref, gain_ref, bias_ref, gatew_ref, gate_ref):
    normed = norm_rows(x_ref[...].reshape(1600, 128).astype(F32), gain_ref[1:2], bias_ref[1:2]).astype(BF16)
    gate = jax.nn.sigmoid(jnp.dot(normed, gatew_ref[1], preferred_element_type=F32))
    gate_ref[...] = gate.reshape(gate_ref.shape)


def last_kernel(own0_ref, own1_ref, own2_ref, other_ref, x_ref, gate_ref, outw_ref, scales_ref, out_ref):
    for s in range(x_ref.shape[0]):
        own = own0_ref[s].astype(F32) + own1_ref[s].astype(F32) + own2_ref[s].astype(F32)
        tri = jnp.concatenate([unpack(own), unpack(other_ref[s])], axis=0)
        upd = norm_chans(tri, wide(scales_ref[2]), wide(scales_ref[3]))
        upd = jnp.transpose(upd)[:160].astype(BF16)
        turned = jnp.dot(upd, outw_ref[...], preferred_element_type=F32)
        out_ref[s] = (x_ref[s].astype(F32) + gate_ref[s] * turned).astype(BF16)


def params():
    return pltpu.CompilerParams(vmem_limit_bytes=VMEM_LIMIT)


def cost(flops, nbytes):
    return pl.CostEstimate(flops=flops, bytes_accessed=nbytes, transcendentals=0)


def whole(shape):
    zeros = (0,) * len(shape)
    return pl.BlockSpec(shape, lambda *_: zeros)


def share_call(info, pair, gain, bias, weight):
    return pl.pallas_call(
        share_kernel,
        grid_spec=pltpu.PrefetchScalarGridSpec(
            num_scalar_prefetch=1,
            grid=(4,),
            in_specs=[
                pl.BlockSpec((5, 160, 128), lambda b, info: (4 * info[0] + b, 0, 0)),
                whole((2, 128)), whole((2, 128)), pl.BlockSpec((1, 128, 512), lambda b, info: (0, 0, 0)),
            ],
            out_specs=pl.BlockSpec(
                (None, 5, 80, 128),
                lambda b, info: (jnp.where(info[1] == 0, b // 2, 1 - b // 2), b % 2, 0, 0),
            ),
            scratch_shapes=[pltpu.VMEM((128, 128), BF16)],
        ),
        out_shape=jax.ShapeDtypeStruct((2, 10, 80, 128), BF16),
        compiler_params=params(),
        name="share",
    )(info, pair, gain, bias, weight)


def tile_call(info, pair, gain, bias, weight):
    return pl.pallas_call(
        tile_kernel,
        grid_spec=pltpu.PrefetchScalarGridSpec(
            num_scalar_prefetch=1,
            grid=(10,),
            in_specs=[
                pl.BlockSpec((16, 160, 128), lambda b, info: (b, 0, 0)),
                whole((2, 128)), whole((2, 128)), pl.BlockSpec((1, 128, 512), lambda b, info: (0, 0, 0)),
            ],
            out_specs=pl.BlockSpec((64, 16, 256), lambda b, info: (0, b, 0)),
            scratch_shapes=[pltpu.VMEM((128, 128), BF16)],
        ),
        out_shape=jax.ShapeDtypeStruct((64, 160, 256), BF16),
        compiler_params=params(),
        cost_estimate=cost(20 * 10**9, 40 * 2**20),
        name="tile",
    )(info, pair, gain, bias, weight)


def contract_call(info, big, small):
    scratch = [
        pltpu.VMEM((80, 80, 128), BF16),
        pltpu.VMEM((64, 80, 128), BF16), pltpu.VMEM((64, 80, 128), BF16),
        pltpu.VMEM((64, 80, 128), BF16), pltpu.VMEM((16, 80, 128), BF16),
    ]
    if len(big) > 1:
        scratch += [
            pltpu.VMEM((160, 80, 128), BF16),
            pltpu.VMEM((64, 160, 128), BF16), pltpu.VMEM((64, 160, 128), BF16),
        ]
    args = list(big) + list(small)
    return pl.pallas_call(
        functools.partial(contract_kernel, len(big), len(small)),
        in_specs=[pl.BlockSpec(memory_space=pltpu.SMEM)] + [pl.BlockSpec(memory_space=pltpu.VMEM)] * len(args),
        out_specs=[pl.BlockSpec(memory_space=pltpu.VMEM)] * 8,
        out_shape=[jax.ShapeDtypeStruct((10, 80, 128), BF16)] * 8,
        scratch_shapes=scratch,
        compiler_params=params(),
        name="contract",
    )(info, *args)


def simple_call(kernel, name, shapes, args, smem=0, flops=10**9):
    vmem = pl.BlockSpec(memory_space=pltpu.VMEM)
    return pl.pallas_call(
        kernel,
        in_specs=[pl.BlockSpec(memory_space=pltpu.SMEM)] * smem + [vmem] * (len(args) - smem),
        out_specs=[vmem] * len(shapes),
        out_shape=[jax.ShapeDtypeStruct(*s) for s in shapes],
        compiler_params=params(),
        cost_estimate=cost(flops, 8 * 2**20),
        name=name,
    )(*args)


def shift_by(values, axis, step):
    n = lax.axis_size(axis)
    return lax.ppermute(values, axis, [(i, (i + step) % n) for i in range(n)])


def swap_cores(values):
    return lax.ppermute(values, "depth", [(d, d ^ 1) for d in range(lax.axis_size("depth"))])


def gather4(values, axis):
    return [values, shift_by(values, axis, -1), shift_by(values, axis, 2), shift_by(values, axis, 1)]


def add2(a, b):
    return (a.astype(F32) + b.astype(F32)).astype(BF16)


def scatter4(parts, axis):
    p0, p1, p2, p3 = (parts[2 * u : 2 * u + 2] for u in range(4))
    up2 = shift_by(p2[0], axis, 1)
    down2 = shift_by(p2[1], axis, -1)
    up1 = shift_by(p1[1], axis, 1)
    down1 = shift_by(p3[0], axis, -1)
    up0 = shift_by(add2(p1[0], up2), axis, 1)
    down0 = shift_by(add2(p3[1], down2), axis, -1)
    return (p0[0], up0, down1), (p0[1], up1, down0)


def ring8(x):
    got = [x] + [None] * 7
    for k in range(1, 4):
        got[8 - k] = shift_by(got[(9 - k) % 8], "depth", 2)
        got[k] = shift_by(got[k - 1], "depth", -2)
    n = x.shape[0] // 2
    got[4] = [shift_by(got[5][:n], "depth", 2), shift_by(got[3][n:], "depth", -2)]
    return got


def on_device(pair, in_gain, in_bias, proj_weight, gate_weight, out_gain, out_bias, out_weight):
    layer = lax.axis_index("depth")
    z, half = layer // 2, layer % 2
    here, there = lax.axis_index("row"), lax.axis_index("col")
    info = jnp.stack([z, half, (here - there + 4) % 4]).astype(jnp.int32)
    info1 = jnp.stack([z, half, (there - here + 4) % 4]).astype(jnp.int32)

    right = share_call(info, pair, in_gain, in_bias, proj_weight)
    right_all = gather4(right, "row")
    left = tile_call(info, pair, in_gain, in_bias, proj_weight)
    columns = lax.dynamic_slice_in_dim(pair, 10 * layer, 10, 1).transpose(1, 0, 2)
    gate, field, proj, out0, out1, scales = simple_call(
        prep_kernel, "prep",
        [((10, 128, 256), F32), ((10, 128, 256), BF16), ((512, 128), BF16), ((128, 128), BF16),
         ((128, 128), BF16), ((6, 128, 128), F32)],
        [info, columns, in_gain, in_bias, proj_weight, gate_weight, out_gain, out_bias, out_weight],
        smem=1,
    )
    own, sent = scatter4(contract_call(info, [left], right_all), "col")
    other = swap_cores(add2(sum(v.astype(F32) for v in sent[:2]), sent[2]))

    packed = ((10, 80, 128), BF16)
    middle, keep_l, keep_r, send_l, send_r = simple_call(
        middle_kernel, "middle", [((10, 160, 128), BF16)] + [packed] * 4,
        [*own, other, gate, field, proj, out0, scales],
    )
    rights = ring8(jnp.stack([keep_r, swap_cores(send_r)]))
    lefts = gather4(jnp.stack([keep_l, swap_cores(send_l)]), "col")
    big = rights[:4] + [v[0] for v in rights[4]] + rights[5:]
    parts = contract_call(info1, big, lefts)
    *parts, middle = lax.optimization_barrier((*parts, middle))
    own, sent = scatter4(parts, "row")
    other = swap_cores(add2(sum(v.astype(F32) for v in sent[:2]), sent[2]))
    moved = lax.all_to_all(middle.reshape(10, 16, 10, 128), "depth", 1, 0, tiled=False)
    rows = moved.reshape(160, 10, 128).transpose(1, 0, 2)
    (gate,) = simple_call(
        gate_kernel, "gate", [((10, 160, 128), F32)], [rows, in_gain, in_bias, gate_weight]
    )
    (result,) = simple_call(
        last_kernel, "last", [((10, 160, 128), BF16)], [*own, other, rows, gate, out1, scales]
    )
    got = ring8(result)
    final = jnp.zeros(pair.shape, BF16)
    for p in (0, 1, 7, 2, 6, 3, 5, 4):
        mine = jnp.concatenate(got[p], axis=0) if p == 4 else got[p]
        place = (z + p) % 8 * 20
        final = lax.dynamic_update_slice(final, mine, (place + 10 * half, 0, 0))
        final = lax.dynamic_update_slice(final, swap_cores(mine), (place + 10 * (1 - half), 0, 0))
    return final


def solution(mesh):
    placed = (P("row", "col", None), P(), P(), P(), P(), P(), P(), P())
    return jax.shard_map(
        on_device, mesh=mesh, in_specs=placed, out_specs=P("row", "col", None), check_vma=False
    )
```

```python
import functools

import jax
import jax.numpy as jnp
from jax import lax
from jax.experimental import pallas as pl
from jax.experimental.pallas import tpu as pltpu
from jax.sharding import PartitionSpec as P

F32 = jnp.float32
BF16 = jnp.bfloat16
VMEM_LIMIT = 60 * 1024 * 1024
NT = (((1,), (1,)), ((), ()))


def norm_block(rows, gain, bias):
    ones = jnp.full((128, 128), 1 / 128, BF16)
    centred = rows.astype(F32) - jnp.dot(rows, ones, preferred_element_type=F32)
    spread = jnp.dot((centred * centred).astype(BF16), ones, preferred_element_type=F32)
    return (centred * lax.rsqrt(spread + 1e-05) * gain + bias).astype(BF16)


def norm_chans(values, gain, bias):
    mean = jnp.mean(values, axis=0, keepdims=True)
    centred = values - mean
    spread = jnp.mean(centred * centred, axis=0, keepdims=True)
    return centred * lax.rsqrt(spread + 1e-05) * gain + bias


def widen_rows(rows):
    return jnp.concatenate([rows, jnp.zeros((256 - rows.shape[0], rows.shape[1]), rows.dtype)], axis=0)


def fold(tail):
    total = tail[:16]
    for m in range(1, 4):
        total = total + pltpu.roll(tail[16 * m : 16 * m + 16], 32 * m, 1)
    return total


def unfold(packed):
    parts = [packed] + [pltpu.roll(packed, 128 - 32 * m, 1) for m in range(1, 4)]
    tail = jnp.concatenate(parts, axis=0)
    lane = lax.broadcasted_iota(jnp.int32, tail.shape, 1)
    return jnp.where(lane < 32, tail, 0.0)


def pack(chans):
    return jnp.concatenate([chans[:, :128], fold(chans[:, 128:])], axis=0).astype(BF16)


def unpack(block):
    wide = block.astype(F32)
    return jnp.concatenate([wide[:64], unfold(wide[64:])], axis=1)


def gated_chans(weight_t, normed):
    hidden = lax.dot_general(weight_t, normed, NT, preferred_element_type=F32)
    n = weight_t.shape[0] // 2
    return jax.nn.sigmoid(hidden[n:]) * hidden[:n]


def swap_major(values):
    return jnp.swapaxes(values, 0, 1)


def pick_weight(weight_ref, half, first):
    both = []
    for start in (first, first + 128):
        pane = weight_ref[0, :, start : start + 128].astype(F32)
        both.append(jnp.where(half == 0, pane[:, :64], pane[:, 64:]))
    return jnp.transpose(jnp.concatenate(both, axis=1)).astype(BF16)


def share_kernel(info_ref, x_ref, gain_ref, bias_ref, weight_ref, out_ref, weight):
    @pl.when(pl.program_id(0) == 0)
    def _():
        weight[...] = pick_weight(weight_ref, info_ref[1], 256)

    per = x_ref.shape[0]
    normed = norm_block(x_ref[...].reshape(per * 160, 128), gain_ref[0:1], bias_ref[0:1])
    for r in range(per):
        out_ref[r] = pack(gated_chans(weight[...], widen_rows(normed[160 * r : 160 * r + 160])))


def tile_kernel(info_ref, x_ref, gain_ref, bias_ref, weight_ref, out_ref, weight):
    @pl.when(pl.program_id(0) == 0)
    def _():
        weight[...] = pick_weight(weight_ref, info_ref[1], 0)

    per = x_ref.shape[0]
    normed = norm_block(x_ref[...].reshape(per * 160, 128), gain_ref[0:1], bias_ref[0:1])
    rows = []
    for r in range(per):
        values = gated_chans(weight[...], normed[160 * r : 160 * r + 160]).astype(BF16)
        rows.append(jnp.concatenate([values, jnp.zeros((64, 96), BF16)], axis=1))
    for side in range(2):
        at = slice(128 * side, 128 * side + 128)
        out_ref[:, :, at] = swap_major(jnp.stack([row[:, at] for row in rows]))


def spread_blocks(blocks, main, tail, groups, mask):
    def step(g, carry):
        at = pl.ds(pl.multiple_of(g * 16, 16), 16)
        x = blocks[at]
        main[:, at, :] = swap_major(x[:, :64])
        folded = swap_major(x[:, 64:]).astype(F32).reshape(256, 128)
        lane = lax.broadcasted_iota(jnp.int32, (256, 128), 1)
        for m in range(4):
            part = folded if m == 0 else pltpu.roll(folded, 128 - 32 * m, 1)
            if mask:
                part = jnp.where(lane < 32, part, 0.0)
            tail[16 * m : 16 * m + 16, at, :] = part.astype(BF16).reshape(16, 16, 128)
        return carry

    lax.fori_loop(0, groups, step, 0)


def contract_kernel(n_big, n_small, info_ref, *refs):
    z, half, shift = info_ref[0], info_ref[1], info_ref[2]
    big_refs, refs = refs[:n_big], refs[n_big:]
    small_refs, refs = refs[:n_small], refs[n_small:]
    out_refs, refs = refs[:8], refs[8:]
    sblk, smain, stail, omain, otail = refs[:5]
    pieces = n_small // 4
    for t in range(4):
        spot = lax.rem(t + shift, 4) * 20
        for s in range(pieces):
            ref = small_refs[t * pieces + s]
            n = ref.shape[1]
            for o in range(2):
                sblk[pl.ds(spot + 10 * o + n * s, n)] = ref[o]
    spread_blocks(sblk, smain, stail, 5, True)
    if n_big > 1:
        bblk, bmain, btail = refs[5:]
        for p in range(8):
            spot = lax.rem(z + p, 8) * 20
            for o in range(2):
                sh = half if o == 0 else 1 - half
                piece = big_refs[p][o] if p < 4 else big_refs[4 + o][...] if p == 4 else big_refs[p + 1][o]
                bblk[pl.ds(spot + 10 * sh, 10)] = piece
        spread_blocks(bblk, bmain, btail, 10, False)

    def multiply(rho, carry):
        ends = []
        for m in range(4):
            c = 16 * m + rho
            small = jnp.concatenate([smain[c], stail[c]], axis=1)
            big = big_refs[0][c] if n_big == 1 else jnp.concatenate([bmain[c], btail[c]], axis=1)
            product = lax.dot_general(small, big, NT, preferred_element_type=F32)
            omain[c] = product[:, :128].astype(BF16)
            ends.append(product[:, 128:])
        otail[rho] = jnp.concatenate(ends, axis=1).astype(BF16)
        return carry

    lax.fori_loop(0, 16, multiply, 0, unroll=4)
    for g in range(5):
        at = slice(16 * g, 16 * g + 16)
        main = swap_major(omain[:, at, :])
        tail = swap_major(otail[:, at, :])
        for r in range(16):
            b = 16 * g + r
            out = out_refs[b // 10]
            out[b % 10, :64] = main[r]
            out[b % 10, 64:] = tail[r]


def turn(values):
    return jnp.transpose(values.astype(F32))


def prep_kernel(
    info_ref, x_ref, gain_ref, bias_ref, projw_ref, gatew_ref, ogain_ref, obias_ref, outw_ref,
    gate_ref, field_ref, proj_ref, out0_ref, out1_ref, scales_ref,
):
    half = info_ref[1]

    def local(values):
        return jnp.where(half == 0, values, jnp.concatenate([values[64:], values[:64]], axis=0))

    def column(row):
        return jnp.transpose(jnp.broadcast_to(row, (128, 128)))

    for s in range(4):
        proj_ref[128 * s : 128 * s + 128] = local(turn(projw_ref[1, :, 128 * s : 128 * s + 128])).astype(BF16)
    rolled = local(outw_ref[0].astype(F32))
    out0_ref[...] = jnp.transpose(rolled).astype(BF16)
    out1_ref[...] = local(outw_ref[1].astype(F32)).astype(BF16)
    for n, row in enumerate((ogain_ref[0:1], obias_ref[0:1], ogain_ref[1:2], obias_ref[1:2])):
        scales_ref[n] = local(column(row))
    scales_ref[4] = column(gain_ref[1:2])
    scales_ref[5] = column(bias_ref[1:2])
    gate_w = turn(gatew_ref[0]).astype(BF16)
    eye = lax.broadcasted_iota(jnp.int32, (128, 128), 0) == lax.broadcasted_iota(jnp.int32, (128, 128), 1)
    eye = eye.astype(F32).astype(BF16)
    normed = norm_block(x_ref[...].reshape(1600, 128), gain_ref[0:1], bias_ref[0:1])
    for s in range(x_ref.shape[0]):
        x = x_ref[s]
        rows = widen_rows(normed[160 * s : 160 * s + 160])
        gate_ref[s] = jax.nn.sigmoid(lax.dot_general(gate_w, rows, NT, preferred_element_type=F32))
        field = lax.dot_general(eye, widen_rows(x), NT, preferred_element_type=F32)
        field_ref[s] = field.astype(BF16)


def wide(scale):
    return jnp.concatenate([scale, scale], axis=1)


def middle_kernel(
    own0_ref, own1_ref, own2_ref, other0_ref, other1_ref, other2_ref, gate_ref, field_ref, proj_ref, outw_ref, scales_ref,
    mid_ref, keepl_ref, keepr_ref, sendl_ref, sendr_ref,
):
    lane = lax.broadcasted_iota(jnp.int32, (128, 256), 1)
    for s in range(gate_ref.shape[0]):
        own = own0_ref[s].astype(F32) + own1_ref[s].astype(F32) + own2_ref[s].astype(F32)
        other = other0_ref[s].astype(F32) + other1_ref[s].astype(F32) + other2_ref[s].astype(F32)
        tri = jnp.concatenate([unpack(own), unpack(other)], axis=0)
        upd = norm_chans(tri, wide(scales_ref[0]), wide(scales_ref[1])).astype(BF16)
        turned = jnp.dot(outw_ref[...], upd, preferred_element_type=F32)
        middle = (field_ref[s].astype(F32) + gate_ref[s] * turned).astype(BF16).astype(F32)
        mid_ref[s] = jnp.transpose(middle)[:160].astype(BF16)
        normed = norm_chans(middle, wide(scales_ref[4]), wide(scales_ref[5])).astype(BF16)
        hidden = jnp.dot(proj_ref[...], normed, preferred_element_type=F32)
        for side, (keep_ref, send_ref) in enumerate(((keepl_ref, sendl_ref), (keepr_ref, sendr_ref))):
            h = hidden[256 * side : 256 * side + 256]
            value = jnp.where(lane < 160, jax.nn.sigmoid(h[128:]) * h[:128], 0.0)
            keep_ref[s] = pack(value[:64])
            send_ref[s] = pack(value[64:])


def gate_kernel(x_ref, gain_ref, bias_ref, gatew_ref, gate_ref):
    normed = norm_block(x_ref[...].reshape(1600, 128), gain_ref[1:2], bias_ref[1:2])
    gate = jax.nn.sigmoid(jnp.dot(normed, gatew_ref[1], preferred_element_type=F32))
    gate_ref[...] = gate.reshape(gate_ref.shape)


def last_kernel(
    own0_ref, own1_ref, own2_ref, other0_ref, other1_ref, other2_ref, x_ref, gate_ref, outw_ref, scales_ref, out_ref
):
    for s in range(x_ref.shape[0]):
        own = own0_ref[s].astype(F32) + own1_ref[s].astype(F32) + own2_ref[s].astype(F32)
        other = other0_ref[s].astype(F32) + other1_ref[s].astype(F32) + other2_ref[s].astype(F32)
        tri = jnp.concatenate([unpack(own), unpack(other)], axis=0)
        upd = norm_chans(tri, wide(scales_ref[2]), wide(scales_ref[3]))
        upd = jnp.transpose(upd)[:160].astype(BF16)
        turned = jnp.dot(upd, outw_ref[...], preferred_element_type=F32)
        out_ref[s] = (x_ref[s].astype(F32) + gate_ref[s] * turned).astype(BF16)


def params():
    return pltpu.CompilerParams(vmem_limit_bytes=VMEM_LIMIT)


def cost(flops, nbytes):
    return pl.CostEstimate(flops=flops, bytes_accessed=nbytes, transcendentals=0)


def whole(shape):
    zeros = (0,) * len(shape)
    return pl.BlockSpec(shape, lambda *_: zeros)


def share_call(info, pair, gain, bias, weight):
    return pl.pallas_call(
        share_kernel,
        grid_spec=pltpu.PrefetchScalarGridSpec(
            num_scalar_prefetch=1,
            grid=(2,),
            in_specs=[
                pl.BlockSpec((10, 160, 128), lambda b, info: (2 * info[0] + b, 0, 0)),
                whole((2, 128)), whole((2, 128)), pl.BlockSpec((1, 128, 512), lambda b, info: (0, 0, 0)),
            ],
            out_specs=pl.BlockSpec(
                (None, 10, 80, 128), lambda b, info: (jnp.where(info[1] == 0, b, 1 - b), 0, 0, 0)
            ),
            scratch_shapes=[pltpu.VMEM((128, 128), BF16)],
        ),
        out_shape=jax.ShapeDtypeStruct((2, 10, 80, 128), BF16),
        compiler_params=params(),
        name="share",
    )(info, pair, gain, bias, weight)


def tile_call(info, pair, gain, bias, weight):
    return pl.pallas_call(
        tile_kernel,
        grid_spec=pltpu.PrefetchScalarGridSpec(
            num_scalar_prefetch=1,
            grid=(5,),
            in_specs=[
                pl.BlockSpec((32, 160, 128), lambda b, info: (b, 0, 0)),
                whole((2, 128)), whole((2, 128)), pl.BlockSpec((1, 128, 512), lambda b, info: (0, 0, 0)),
            ],
            out_specs=pl.BlockSpec((64, 32, 256), lambda b, info: (0, b, 0)),
            scratch_shapes=[pltpu.VMEM((128, 128), BF16)],
        ),
        out_shape=jax.ShapeDtypeStruct((64, 160, 256), BF16),
        compiler_params=params(),
        cost_estimate=cost(20 * 10**9, 40 * 2**20),
        name="tile",
    )(info, pair, gain, bias, weight)


def contract_call(info, big, small):
    scratch = [
        pltpu.VMEM((80, 80, 128), BF16),
        pltpu.VMEM((64, 80, 128), BF16), pltpu.VMEM((64, 80, 128), BF16),
        pltpu.VMEM((64, 80, 128), BF16), pltpu.VMEM((16, 80, 128), BF16),
    ]
    if len(big) > 1:
        scratch += [
            pltpu.VMEM((160, 80, 128), BF16),
            pltpu.VMEM((64, 160, 128), BF16), pltpu.VMEM((64, 160, 128), BF16),
        ]
    args = list(big) + list(small)
    return pl.pallas_call(
        functools.partial(contract_kernel, len(big), len(small)),
        in_specs=[pl.BlockSpec(memory_space=pltpu.SMEM)] + [pl.BlockSpec(memory_space=pltpu.VMEM)] * len(args),
        out_specs=[pl.BlockSpec(memory_space=pltpu.VMEM)] * 8,
        out_shape=[jax.ShapeDtypeStruct((10, 80, 128), BF16)] * 8,
        scratch_shapes=scratch,
        compiler_params=params(),
        cost_estimate=cost(30 * 10**9, 60 * 2**20),
        name="contract",
    )(info, *args)


def simple_call(kernel, name, shapes, args, smem=0, flops=10**9):
    vmem = pl.BlockSpec(memory_space=pltpu.VMEM)
    return pl.pallas_call(
        kernel,
        in_specs=[pl.BlockSpec(memory_space=pltpu.SMEM)] * smem + [vmem] * (len(args) - smem),
        out_specs=[vmem] * len(shapes),
        out_shape=[jax.ShapeDtypeStruct(*s) for s in shapes],
        compiler_params=params(),
        cost_estimate=cost(flops, 8 * 2**20),
        name=name,
    )(*args)


def shift_by(values, axis, step):
    n = lax.axis_size(axis)
    return lax.ppermute(values, axis, [(i, (i + step) % n) for i in range(n)])


def swap_cores(values):
    return lax.ppermute(values, "depth", [(d, d ^ 1) for d in range(lax.axis_size("depth"))])


def gather4(values, axis):
    return [values, shift_by(values, axis, -1), shift_by(values, axis, 2), shift_by(values, axis, 1)]


def add2(a, b):
    return (a.astype(F32) + b.astype(F32)).astype(BF16)


def cross_by(values, axis, step):
    n, depth = lax.axis_size(axis), lax.axis_size("depth")
    pairs = [(i * depth + d, (i + step) % n * depth + (d ^ 1)) for i in range(n) for d in range(depth)]
    return lax.ppermute(values, (axis, "depth"), pairs)


def scatter4(parts, axis):
    p0, p1, p2, p3 = (parts[2 * u : 2 * u + 2] for u in range(4))
    up2 = shift_by(p2[0], axis, 1)
    down2 = shift_by(p2[1], axis, -1)
    up1 = cross_by(p1[1], axis, 1)
    down1 = shift_by(p3[0], axis, -1)
    up0 = shift_by(add2(p1[0], up2), axis, 1)
    down0 = cross_by(add2(p3[1], down2), axis, -1)
    return p0[0], up0, down1, swap_cores(p0[1]), up1, down0


def ring8(x, axis=0, beside=()):
    got = [x] + [None] * 7
    for k in range(1, 4):
        if k == 3 and beside:
            got[6], got[2], *beside = lax.optimization_barrier((got[6], got[2], *beside))
        got[8 - k] = shift_by(got[(9 - k) % 8], "depth", 2)
        got[k] = shift_by(got[k - 1], "depth", -2)
    first, second = jnp.split(got[5], 2, axis)[0], jnp.split(got[3], 2, axis)[1]
    got[4] = [shift_by(first, "depth", 2), shift_by(second, "depth", -2)]
    return got, beside


def assemble_kernel(first, steps, info_ref, *refs):
    out_ref, sem = refs[-2], refs[-1]
    pieces = refs[: 2 * len(steps)] if first else refs[1:-2]
    z, half = info_ref[0], info_ref[1]
    copies = []
    for n, ref in enumerate(pieces):
        p, side = steps[n // 2], n % 2
        core = half if side == 0 else 1 - half
        row = lax.rem(z + p, 8) * 20 + 10 * core
        copies.append(pltpu.make_async_copy(ref, out_ref.at[pl.ds(row, 10)], sem.at[n]))
    for copy in copies:
        copy.start()
    for copy in copies:
        copy.wait()


def assemble_call(info, steps, pieces, base=None):
    anywhere = pl.BlockSpec(memory_space=pl.ANY)
    args = [info] + ([] if base is None else [base]) + list(pieces)
    return pl.pallas_call(
        functools.partial(assemble_kernel, base is None, steps),
        in_specs=(
            [pl.BlockSpec(memory_space=pltpu.SMEM)]
            + [anywhere] * (base is not None)
            + [pl.BlockSpec(memory_space=pltpu.VMEM)] * len(pieces)
        ),
        out_specs=anywhere,
        out_shape=jax.ShapeDtypeStruct((160, 160, 128), BF16),
        scratch_shapes=[pltpu.SemaphoreType.DMA((len(pieces),))],
        input_output_aliases={} if base is None else {1: 0},
        compiler_params=params(),
        name="assemble",
    )(*args)


def on_device(pair, in_gain, in_bias, proj_weight, gate_weight, out_gain, out_bias, out_weight):
    layer = lax.axis_index("depth")
    z, half = layer // 2, layer % 2
    here, there = lax.axis_index("row"), lax.axis_index("col")
    info = jnp.stack([z, half, (here - there + 4) % 4]).astype(jnp.int32)
    info1 = jnp.stack([z, half, (there - here + 4) % 4]).astype(jnp.int32)

    right = share_call(info, pair, in_gain, in_bias, proj_weight)
    right_all = gather4(right, "row")
    left = tile_call(info, pair, in_gain, in_bias, proj_weight)
    columns = lax.dynamic_slice_in_dim(pair, 10 * layer, 10, 1).transpose(1, 0, 2)
    gate, field, proj, out0, out1, scales = simple_call(
        prep_kernel, "prep",
        [((10, 128, 256), F32), ((10, 128, 256), BF16), ((512, 128), BF16), ((128, 128), BF16),
         ((128, 128), BF16), ((6, 128, 128), F32)],
        [info, columns, in_gain, in_bias, proj_weight, gate_weight, out_gain, out_bias, out_weight],
        smem=1,
    )
    right_all[3], gate = lax.optimization_barrier((right_all[3], gate))
    addends = scatter4(contract_call(info, [left], right_all), "col")

    packed = ((10, 80, 128), BF16)
    middle, keep_l, keep_r, send_l, send_r = simple_call(
        middle_kernel, "middle", [((10, 160, 128), BF16)] + [packed] * 4,
        [*addends, gate, field, proj, out0, scales],
    )
    rights = jnp.stack([keep_r, swap_cores(send_r)])
    lefts = gather4(jnp.stack([keep_l, swap_cores(send_l)]), "col")
    rights, _ = ring8(rights)
    big = rights[:4] + [v[0] for v in rights[4]] + rights[5:]
    parts = contract_call(info1, big, lefts)
    addends = scatter4(parts, "row")
    moved = lax.all_to_all(middle.reshape(10, 16, 10, 128), "depth", 1, 0, tiled=False)
    rows = moved.reshape(160, 10, 128).transpose(1, 0, 2)
    (gate,) = simple_call(
        gate_kernel, "gate", [((10, 160, 128), F32)], [rows, in_gain, in_bias, gate_weight]
    )
    (result,) = simple_call(
        last_kernel, "last", [((10, 160, 128), BF16)], [*addends, rows, gate, out1, scales]
    )
    got, _ = ring8(result)
    got[4] = jnp.concatenate(got[4], axis=0)
    final = jnp.zeros(pair.shape, BF16)
    for p in (0, 1, 7, 2, 6, 3, 5, 4):
        place = (z + p) % 8 * 20
        final = lax.dynamic_update_slice(final, got[p], (place + 10 * half, 0, 0))
        final = lax.dynamic_update_slice(final, swap_cores(got[p]), (place + 10 * (1 - half), 0, 0))
    return final


def solution(mesh):
    placed = (P("row", "col", None), P(), P(), P(), P(), P(), P(), P())
    return jax.shard_map(
        on_device, mesh=mesh, in_specs=placed, out_specs=P("row", "col", None), check_vma=False
    )
```

```python
import functools

import jax
import jax.numpy as jnp
from jax import lax
from jax.experimental import pallas as pl
from jax.experimental.pallas import tpu as pltpu
from jax.sharding import PartitionSpec as P

F32 = jnp.float32
BF16 = jnp.bfloat16
VMEM_LIMIT = 60 * 1024 * 1024
NT = (((1,), (1,)), ((), ()))


def norm_block(rows, gain, bias):
    ones = jnp.full((128, 128), 1 / 128, BF16)
    centred = rows.astype(F32) - jnp.dot(rows, ones, preferred_element_type=F32)
    spread = jnp.dot((centred * centred).astype(BF16), ones, preferred_element_type=F32)
    return (centred * lax.rsqrt(spread + 1e-05) * gain + bias).astype(BF16)


def norm_chans(values, gain, bias):
    mean = jnp.mean(values, axis=0, keepdims=True)
    centred = values - mean
    spread = jnp.mean(centred * centred, axis=0, keepdims=True)
    return centred * lax.rsqrt(spread + 1e-05) * gain + bias


def widen_rows(rows):
    return jnp.concatenate([rows, jnp.zeros((256 - rows.shape[0], rows.shape[1]), rows.dtype)], axis=0)


def fold(tail):
    total = tail[:16]
    for m in range(1, 4):
        total = total + pltpu.roll(tail[16 * m : 16 * m + 16], 32 * m, 1)
    return total


def unfold(packed):
    parts = [packed] + [pltpu.roll(packed, 128 - 32 * m, 1) for m in range(1, 4)]
    tail = jnp.concatenate(parts, axis=0)
    lane = lax.broadcasted_iota(jnp.int32, tail.shape, 1)
    return jnp.where(lane < 32, tail, 0.0)


def pack(chans):
    return jnp.concatenate([chans[:, :128], fold(chans[:, 128:])], axis=0).astype(BF16)


def unpack(block):
    wide = block.astype(F32)
    return jnp.concatenate([wide[:64], unfold(wide[64:])], axis=1)


def gated_chans(weight_t, normed):
    hidden = lax.dot_general(weight_t, normed, NT, preferred_element_type=F32)
    n = weight_t.shape[0] // 2
    return jax.nn.sigmoid(hidden[n:]) * hidden[:n]


def swap_major(values):
    return jnp.swapaxes(values, 0, 1)


def pick_weight(weight_ref, half, first):
    both = []
    for start in (first, first + 128):
        pane = weight_ref[0, :, start : start + 128].astype(F32)
        both.append(jnp.where(half == 0, pane[:, :64], pane[:, 64:]))
    return jnp.transpose(jnp.concatenate(both, axis=1)).astype(BF16)


def share_kernel(info_ref, x_ref, gain_ref, bias_ref, weight_ref, out_ref, weight):
    @pl.when(pl.program_id(0) == 0)
    def _():
        weight[...] = pick_weight(weight_ref, info_ref[1], 256)

    per = x_ref.shape[0]
    normed = norm_block(x_ref[...].reshape(per * 160, 128), gain_ref[0:1], bias_ref[0:1])
    for r in range(per):
        out_ref[r] = pack(gated_chans(weight[...], widen_rows(normed[160 * r : 160 * r + 160])))


def tile_kernel(info_ref, x_ref, gain_ref, bias_ref, weight_ref, out_ref, weight):
    @pl.when(pl.program_id(0) == 0)
    def _():
        weight[...] = pick_weight(weight_ref, info_ref[1], 0)

    per = x_ref.shape[0]
    normed = norm_block(x_ref[...].reshape(per * 160, 128), gain_ref[0:1], bias_ref[0:1])
    rows = []
    for r in range(per):
        values = gated_chans(weight[...], normed[160 * r : 160 * r + 160]).astype(BF16)
        rows.append(jnp.concatenate([values, jnp.zeros((64, 96), BF16)], axis=1))
    for side in range(2):
        at = slice(128 * side, 128 * side + 128)
        out_ref[:, :, at] = swap_major(jnp.stack([row[:, at] for row in rows]))


def spread_blocks(blocks, main, tail, groups, mask):
    def step(g, carry):
        at = pl.ds(pl.multiple_of(g * 16, 16), 16)
        x = blocks[at]
        main[:, at, :] = swap_major(x[:, :64])
        folded = swap_major(x[:, 64:]).astype(F32).reshape(256, 128)
        lane = lax.broadcasted_iota(jnp.int32, (256, 128), 1)
        for m in range(4):
            part = folded if m == 0 else pltpu.roll(folded, 128 - 32 * m, 1)
            if mask:
                part = jnp.where(lane < 32, part, 0.0)
            tail[16 * m : 16 * m + 16, at, :] = part.astype(BF16).reshape(16, 16, 128)
        return carry

    lax.fori_loop(0, groups, step, 0)


def contract_kernel(n_big, n_small, info_ref, *refs):
    z, half, shift = info_ref[0], info_ref[1], info_ref[2]
    big_refs, refs = refs[:n_big], refs[n_big:]
    small_refs, refs = refs[:n_small], refs[n_small:]
    out_refs, refs = refs[:8], refs[8:]
    sblk, smain, stail, omain, otail = refs[:5]
    pieces = n_small // 4
    for t in range(4):
        spot = lax.rem(t + shift, 4) * 20
        for s in range(pieces):
            ref = small_refs[t * pieces + s]
            n = ref.shape[1]
            for o in range(2):
                sblk[pl.ds(spot + 10 * o + n * s, n)] = ref[o]
    spread_blocks(sblk, smain, stail, 5, True)
    if n_big > 1:
        bblk, bmain, btail = refs[5:]
        for p in range(8):
            spot = lax.rem(z + p, 8) * 20
            for o in range(2):
                sh = half if o == 0 else 1 - half
                piece = big_refs[p][o] if p < 4 else big_refs[4 + o][...] if p == 4 else big_refs[p + 1][o]
                bblk[pl.ds(spot + 10 * sh, 10)] = piece
        spread_blocks(bblk, bmain, btail, 10, False)

    def multiply(rho, carry):
        ends = []
        for m in range(4):
            c = 16 * m + rho
            small = jnp.concatenate([smain[c], stail[c]], axis=1)
            big = big_refs[0][c] if n_big == 1 else jnp.concatenate([bmain[c], btail[c]], axis=1)
            product = lax.dot_general(small, big, NT, preferred_element_type=F32)
            omain[c] = product[:, :128].astype(BF16)
            ends.append(product[:, 128:])
        otail[rho] = jnp.concatenate(ends, axis=1).astype(BF16)
        return carry

    lax.fori_loop(0, 16, multiply, 0, unroll=4)
    for g in range(5):
        at = slice(16 * g, 16 * g + 16)
        main = swap_major(omain[:, at, :])
        tail = swap_major(otail[:, at, :])
        for r in range(16):
            b = 16 * g + r
            out = out_refs[b // 10]
            out[b % 10, :64] = main[r]
            out[b % 10, 64:] = tail[r]


def turn(values):
    return jnp.transpose(values.astype(F32))


def prep_kernel(
    info_ref, x_ref, gain_ref, bias_ref, projw_ref, gatew_ref, ogain_ref, obias_ref, outw_ref,
    gate_ref, field_ref, proj_ref, out0_ref, out1_ref, scales_ref,
):
    half = info_ref[1]

    def local(values):
        return jnp.where(half == 0, values, jnp.concatenate([values[64:], values[:64]], axis=0))

    def column(row):
        return jnp.transpose(jnp.broadcast_to(row, (128, 128)))

    for s in range(4):
        proj_ref[128 * s : 128 * s + 128] = local(turn(projw_ref[1, :, 128 * s : 128 * s + 128])).astype(BF16)
    rolled = local(outw_ref[0].astype(F32))
    out0_ref[...] = jnp.transpose(rolled).astype(BF16)
    out1_ref[...] = local(outw_ref[1].astype(F32)).astype(BF16)
    for n, row in enumerate((ogain_ref[0:1], obias_ref[0:1], ogain_ref[1:2], obias_ref[1:2])):
        scales_ref[n] = local(column(row))
    scales_ref[4] = column(gain_ref[1:2])
    scales_ref[5] = column(bias_ref[1:2])
    gate_w = turn(gatew_ref[0]).astype(BF16)
    eye = lax.broadcasted_iota(jnp.int32, (128, 128), 0) == lax.broadcasted_iota(jnp.int32, (128, 128), 1)
    eye = eye.astype(F32).astype(BF16)
    normed = norm_block(x_ref[...].reshape(1600, 128), gain_ref[0:1], bias_ref[0:1])
    for s in range(x_ref.shape[0]):
        x = x_ref[s]
        rows = widen_rows(normed[160 * s : 160 * s + 160])
        gate_ref[s] = jax.nn.sigmoid(lax.dot_general(gate_w, rows, NT, preferred_element_type=F32))
        field = lax.dot_general(eye, widen_rows(x), NT, preferred_element_type=F32)
        field_ref[s] = field.astype(BF16)


def wide(scale):
    return jnp.concatenate([scale, scale], axis=1)


def middle_kernel(
    own0_ref, own1_ref, own2_ref, other0_ref, other1_ref, other2_ref, gate_ref, field_ref, proj_ref, outw_ref, scales_ref,
    mid_ref, keepl_ref, keepr_ref, sendl_ref, sendr_ref,
):
    lane = lax.broadcasted_iota(jnp.int32, (128, 256), 1)
    for s in range(gate_ref.shape[0]):
        own = own0_ref[s].astype(F32) + own1_ref[s].astype(F32) + own2_ref[s].astype(F32)
        other = other0_ref[s].astype(F32) + other1_ref[s].astype(F32) + other2_ref[s].astype(F32)
        tri = jnp.concatenate([unpack(own), unpack(other)], axis=0)
        upd = norm_chans(tri, wide(scales_ref[0]), wide(scales_ref[1])).astype(BF16)
        turned = jnp.dot(outw_ref[...], upd, preferred_element_type=F32)
        middle = (field_ref[s].astype(F32) + gate_ref[s] * turned).astype(BF16).astype(F32)
        mid_ref[s] = jnp.transpose(middle)[:160].astype(BF16)
        normed = norm_chans(middle, wide(scales_ref[4]), wide(scales_ref[5])).astype(BF16)
        hidden = jnp.dot(proj_ref[...], normed, preferred_element_type=F32)
        for side, (keep_ref, send_ref) in enumerate(((keepl_ref, sendl_ref), (keepr_ref, sendr_ref))):
            h = hidden[256 * side : 256 * side + 256]
            value = jnp.where(lane < 160, jax.nn.sigmoid(h[128:]) * h[:128], 0.0)
            keep_ref[s] = pack(value[:64])
            send_ref[s] = pack(value[64:])


def gate_kernel(x_ref, gain_ref, bias_ref, gatew_ref, gate_ref):
    normed = norm_block(x_ref[...].reshape(1600, 128), gain_ref[1:2], bias_ref[1:2])
    gate = jax.nn.sigmoid(jnp.dot(normed, gatew_ref[1], preferred_element_type=F32))
    gate_ref[...] = gate.reshape(gate_ref.shape)


def last_kernel(
    own0_ref, own1_ref, own2_ref, other0_ref, other1_ref, other2_ref, x_ref, gate_ref, outw_ref, scales_ref, out_ref
):
    for s in range(x_ref.shape[0]):
        own = own0_ref[s].astype(F32) + own1_ref[s].astype(F32) + own2_ref[s].astype(F32)
        other = other0_ref[s].astype(F32) + other1_ref[s].astype(F32) + other2_ref[s].astype(F32)
        tri = jnp.concatenate([unpack(own), unpack(other)], axis=0)
        upd = norm_chans(tri, wide(scales_ref[2]), wide(scales_ref[3]))
        upd = jnp.transpose(upd)[:160].astype(BF16)
        turned = jnp.dot(upd, outw_ref[...], preferred_element_type=F32)
        out_ref[s] = (x_ref[s].astype(F32) + gate_ref[s] * turned).astype(BF16)


def params():
    return pltpu.CompilerParams(vmem_limit_bytes=VMEM_LIMIT)


def cost(flops, nbytes):
    return pl.CostEstimate(flops=flops, bytes_accessed=nbytes, transcendentals=0)


def whole(shape):
    zeros = (0,) * len(shape)
    return pl.BlockSpec(shape, lambda *_: zeros)


def share_call(info, pair, gain, bias, weight):
    return pl.pallas_call(
        share_kernel,
        grid_spec=pltpu.PrefetchScalarGridSpec(
            num_scalar_prefetch=1,
            grid=(2,),
            in_specs=[
                pl.BlockSpec((10, 160, 128), lambda b, info: (2 * info[0] + b, 0, 0)),
                whole((2, 128)), whole((2, 128)), pl.BlockSpec((1, 128, 512), lambda b, info: (0, 0, 0)),
            ],
            out_specs=pl.BlockSpec(
                (None, 10, 80, 128), lambda b, info: (jnp.where(info[1] == 0, b, 1 - b), 0, 0, 0)
            ),
            scratch_shapes=[pltpu.VMEM((128, 128), BF16)],
        ),
        out_shape=jax.ShapeDtypeStruct((2, 10, 80, 128), BF16),
        compiler_params=params(),
        name="share",
    )(info, pair, gain, bias, weight)


def tile_call(info, pair, gain, bias, weight):
    return pl.pallas_call(
        tile_kernel,
        grid_spec=pltpu.PrefetchScalarGridSpec(
            num_scalar_prefetch=1,
            grid=(5,),
            in_specs=[
                pl.BlockSpec((32, 160, 128), lambda b, info: (b, 0, 0)),
                whole((2, 128)), whole((2, 128)), pl.BlockSpec((1, 128, 512), lambda b, info: (0, 0, 0)),
            ],
            out_specs=pl.BlockSpec((64, 32, 256), lambda b, info: (0, b, 0)),
            scratch_shapes=[pltpu.VMEM((128, 128), BF16)],
        ),
        out_shape=jax.ShapeDtypeStruct((64, 160, 256), BF16),
        compiler_params=params(),
        cost_estimate=cost(20 * 10**9, 40 * 2**20),
        name="tile",
    )(info, pair, gain, bias, weight)


def contract_call(info, big, small):
    scratch = [
        pltpu.VMEM((80, 80, 128), BF16),
        pltpu.VMEM((64, 80, 128), BF16), pltpu.VMEM((64, 80, 128), BF16),
        pltpu.VMEM((64, 80, 128), BF16), pltpu.VMEM((16, 80, 128), BF16),
    ]
    if len(big) > 1:
        scratch += [
            pltpu.VMEM((160, 80, 128), BF16),
            pltpu.VMEM((64, 160, 128), BF16), pltpu.VMEM((64, 160, 128), BF16),
        ]
    args = list(big) + list(small)
    return pl.pallas_call(
        functools.partial(contract_kernel, len(big), len(small)),
        in_specs=[pl.BlockSpec(memory_space=pltpu.SMEM)] + [pl.BlockSpec(memory_space=pltpu.VMEM)] * len(args),
        out_specs=[pl.BlockSpec(memory_space=pltpu.VMEM)] * 8,
        out_shape=[jax.ShapeDtypeStruct((10, 80, 128), BF16)] * 8,
        scratch_shapes=scratch,
        compiler_params=params(),
        cost_estimate=cost(30 * 10**9, 60 * 2**20),
        name="contract",
    )(info, *args)


def simple_call(kernel, name, shapes, args, smem=0, flops=10**9):
    vmem = pl.BlockSpec(memory_space=pltpu.VMEM)
    return pl.pallas_call(
        kernel,
        in_specs=[pl.BlockSpec(memory_space=pltpu.SMEM)] * smem + [vmem] * (len(args) - smem),
        out_specs=[vmem] * len(shapes),
        out_shape=[jax.ShapeDtypeStruct(*s) for s in shapes],
        compiler_params=params(),
        cost_estimate=cost(flops, 8 * 2**20),
        name=name,
    )(*args)


def shift_by(values, axis, step):
    n = lax.axis_size(axis)
    return lax.ppermute(values, axis, [(i, (i + step) % n) for i in range(n)])


def swap_cores(values):
    return lax.ppermute(values, "depth", [(d, d ^ 1) for d in range(lax.axis_size("depth"))])


def gather4(values, axis):
    return [values, shift_by(values, axis, -1), shift_by(values, axis, 2), shift_by(values, axis, 1)]


def add2(a, b):
    return (a.astype(F32) + b.astype(F32)).astype(BF16)


def cross_by(values, axis, step):
    n, depth = lax.axis_size(axis), lax.axis_size("depth")
    pairs = [(i * depth + d, (i + step) % n * depth + (d ^ 1)) for i in range(n) for d in range(depth)]
    return lax.ppermute(values, (axis, "depth"), pairs)


def scatter4(parts, axis):
    p0, p1, p2, p3 = (parts[2 * u : 2 * u + 2] for u in range(4))
    up2 = shift_by(p2[0], axis, 1)
    down2 = shift_by(p2[1], axis, -1)
    up1 = cross_by(p1[1], axis, 1)
    down1 = shift_by(p3[0], axis, -1)
    up0 = shift_by(add2(p1[0], up2), axis, 1)
    down0 = cross_by(add2(p3[1], down2), axis, -1)
    return p0[0], up0, down1, swap_cores(p0[1]), up1, down0


def ring8(x, axis=0, beside=()):
    got = [x] + [None] * 7
    for k in range(1, 4):
        if k == 3 and beside:
            got[6], got[2], *beside = lax.optimization_barrier((got[6], got[2], *beside))
        got[8 - k] = shift_by(got[(9 - k) % 8], "depth", 2)
        got[k] = shift_by(got[k - 1], "depth", -2)
    first, second = jnp.split(got[5], 2, axis)[0], jnp.split(got[3], 2, axis)[1]
    got[4] = [shift_by(first, "depth", 2), shift_by(second, "depth", -2)]
    return got, beside


def assemble_kernel(first, steps, info_ref, *refs):
    out_ref, sem = refs[-2], refs[-1]
    pieces = refs[: 2 * len(steps)] if first else refs[1:-2]
    z, half = info_ref[0], info_ref[1]
    copies = []
    for n, ref in enumerate(pieces):
        p, side = steps[n // 2], n % 2
        core = half if side == 0 else 1 - half
        row = lax.rem(z + p, 8) * 20 + 10 * core
        copies.append(pltpu.make_async_copy(ref, out_ref.at[pl.ds(row, 10)], sem.at[n]))
    for copy in copies:
        copy.start()
    for copy in copies:
        copy.wait()


def assemble_call(info, steps, pieces, base=None):
    anywhere = pl.BlockSpec(memory_space=pl.ANY)
    args = [info] + ([] if base is None else [base]) + list(pieces)
    return pl.pallas_call(
        functools.partial(assemble_kernel, base is None, steps),
        in_specs=(
            [pl.BlockSpec(memory_space=pltpu.SMEM)]
            + [anywhere] * (base is not None)
            + [pl.BlockSpec(memory_space=pltpu.VMEM)] * len(pieces)
        ),
        out_specs=anywhere,
        out_shape=jax.ShapeDtypeStruct((160, 160, 128), BF16),
        scratch_shapes=[pltpu.SemaphoreType.DMA((len(pieces),))],
        input_output_aliases={} if base is None else {1: 0},
        compiler_params=params(),
        name="assemble",
    )(*args)


def on_device(pair, in_gain, in_bias, proj_weight, gate_weight, out_gain, out_bias, out_weight):
    layer = lax.axis_index("depth")
    z, half = layer // 2, layer % 2
    here, there = lax.axis_index("row"), lax.axis_index("col")
    info = jnp.stack([z, half, (here - there + 4) % 4]).astype(jnp.int32)
    info1 = jnp.stack([z, half, (there - here + 4) % 4]).astype(jnp.int32)

    same_core = [list(range(c, 16, 2)) for c in range(2)]

    right = share_call(info, pair, in_gain, in_bias, proj_weight)
    right_all = gather4(right, "row")
    left = tile_call(info, pair, in_gain, in_bias, proj_weight)
    columns = lax.dynamic_slice_in_dim(pair, 10 * layer, 10, 1).transpose(1, 0, 2)
    gate, field, proj, out0, out1, scales = simple_call(
        prep_kernel, "prep",
        [((10, 128, 256), F32), ((10, 128, 256), BF16), ((512, 128), BF16), ((128, 128), BF16),
         ((128, 128), BF16), ((6, 128, 128), F32)],
        [info, columns, in_gain, in_bias, proj_weight, gate_weight, out_gain, out_bias, out_weight],
        smem=1,
    )
    right_all[3], gate = lax.optimization_barrier((right_all[3], gate))
    addends = scatter4(contract_call(info, [left], right_all), "col")

    packed = ((10, 80, 128), BF16)
    middle, keep_l, keep_r, send_l, send_r = simple_call(
        middle_kernel, "middle", [((10, 160, 128), BF16)] + [packed] * 4,
        [*addends, gate, field, proj, out0, scales],
    )
    rights = jnp.stack([keep_r, swap_cores(send_r)])
    lefts = gather4(jnp.stack([keep_l, swap_cores(send_l)]), "col")
    rights, _ = ring8(rights)
    big = rights[:4] + [v[0] for v in rights[4]] + rights[5:]
    parts = contract_call(info1, big, lefts)
    addends = scatter4(parts, "row")
    moved = lax.all_to_all(
        middle.reshape(10, 8, 20, 128), "depth", 1, 0, axis_index_groups=same_core, tiled=False
    )
    own_rows = lax.dynamic_slice_in_dim(moved, 10 * half, 10, 2)
    got_rows = swap_cores(lax.dynamic_slice_in_dim(moved, 10 * (1 - half), 10, 2))
    first, second = jnp.where(half == 0, own_rows, got_rows), jnp.where(half == 0, got_rows, own_rows)
    rows = jnp.stack([first, second], axis=1).reshape(160, 10, 128).transpose(1, 0, 2)
    (gate,) = simple_call(
        gate_kernel, "gate", [((10, 160, 128), F32)], [rows, in_gain, in_bias, gate_weight]
    )
    (result,) = simple_call(
        last_kernel, "last", [((10, 160, 128), BF16)], [*addends, rows, gate, out1, scales]
    )
    got, _ = ring8(result)
    got[4] = jnp.concatenate(got[4], axis=0)
    final = jnp.zeros(pair.shape, BF16)
    for p in (0, 1, 7, 2, 6, 3, 5, 4):
        place = (z + p) % 8 * 20
        final = lax.dynamic_update_slice(final, got[p], (place + 10 * half, 0, 0))
        final = lax.dynamic_update_slice(final, swap_cores(got[p]), (place + 10 * (1 - half), 0, 0))
    return final


def solution(mesh):
    placed = (P("row", "col", None), P(), P(), P(), P(), P(), P(), P())
    return jax.shard_map(
        on_device, mesh=mesh, in_specs=placed, out_specs=P("row", "col", None), check_vma=False
    )
```

```python
import functools

import jax
import jax.numpy as jnp
from jax import lax
from jax.experimental import pallas as pl
from jax.experimental.pallas import tpu as pltpu
from jax.sharding import PartitionSpec as P

F32 = jnp.float32
BF16 = jnp.bfloat16
VMEM_LIMIT = 60 * 1024 * 1024
NT = (((1,), (1,)), ((), ()))


def norm_block(rows, gain, bias):
    ones = jnp.full((128, 128), 1 / 128, BF16)
    centred = rows.astype(F32) - jnp.dot(rows, ones, preferred_element_type=F32)
    spread = jnp.dot((centred * centred).astype(BF16), ones, preferred_element_type=F32)
    return (centred * lax.rsqrt(spread + 1e-05) * gain + bias).astype(BF16)


def norm_chans(values, gain, bias):
    mean = jnp.mean(values, axis=0, keepdims=True)
    centred = values - mean
    spread = jnp.mean(centred * centred, axis=0, keepdims=True)
    return centred * lax.rsqrt(spread + 1e-05) * gain + bias


def widen_rows(rows):
    return jnp.concatenate([rows, jnp.zeros((256 - rows.shape[0], rows.shape[1]), rows.dtype)], axis=0)


def fold(tail):
    total = tail[:16]
    for m in range(1, 4):
        total = total + pltpu.roll(tail[16 * m : 16 * m + 16], 32 * m, 1)
    return total


def unfold(packed):
    parts = [packed] + [pltpu.roll(packed, 128 - 32 * m, 1) for m in range(1, 4)]
    tail = jnp.concatenate(parts, axis=0)
    lane = lax.broadcasted_iota(jnp.int32, tail.shape, 1)
    return jnp.where(lane < 32, tail, 0.0)


def pack(chans):
    return jnp.concatenate([chans[:, :128], fold(chans[:, 128:])], axis=0).astype(BF16)


def unpack(block):
    wide = block.astype(F32)
    return jnp.concatenate([wide[:64], unfold(wide[64:])], axis=1)


def gated_chans(weight_t, normed):
    hidden = lax.dot_general(weight_t, normed, NT, preferred_element_type=F32)
    n = weight_t.shape[0] // 2
    return jax.nn.sigmoid(hidden[n:]) * hidden[:n]


def swap_major(values):
    return jnp.swapaxes(values, 0, 1)


def pick_weight(weight_ref, half, first):
    both = []
    for start in (first, first + 128):
        pane = weight_ref[0, :, start : start + 128].astype(F32)
        both.append(jnp.where(half == 0, pane[:, :64], pane[:, 64:]))
    return jnp.transpose(jnp.concatenate(both, axis=1)).astype(BF16)


def share_kernel(info_ref, x_ref, gain_ref, bias_ref, weight_ref, out_ref, weight):
    @pl.when(pl.program_id(0) == 0)
    def _():
        weight[...] = pick_weight(weight_ref, info_ref[1], 256)

    per = x_ref.shape[0]
    normed = norm_block(x_ref[...].reshape(per * 160, 128), gain_ref[0:1], bias_ref[0:1])
    for r in range(per):
        out_ref[r] = pack(gated_chans(weight[...], widen_rows(normed[160 * r : 160 * r + 160])))


def tile_kernel(info_ref, x_ref, gain_ref, bias_ref, weight_ref, out_ref, weight):
    @pl.when(pl.program_id(0) == 0)
    def _():
        weight[...] = pick_weight(weight_ref, info_ref[1], 0)

    per = x_ref.shape[0]
    normed = norm_block(x_ref[...].reshape(per * 160, 128), gain_ref[0:1], bias_ref[0:1])
    rows = []
    for r in range(per):
        values = gated_chans(weight[...], normed[160 * r : 160 * r + 160]).astype(BF16)
        rows.append(jnp.concatenate([values, jnp.zeros((64, 96), BF16)], axis=1))
    for side in range(2):
        at = slice(128 * side, 128 * side + 128)
        out_ref[:, :, at] = swap_major(jnp.stack([row[:, at] for row in rows]))


def spread_blocks(blocks, main, tail, groups, mask):
    def step(g, carry):
        at = pl.ds(pl.multiple_of(g * 16, 16), 16)
        x = blocks[at]
        main[:, at, :] = swap_major(x[:, :64])
        folded = swap_major(x[:, 64:]).astype(F32).reshape(256, 128)
        lane = lax.broadcasted_iota(jnp.int32, (256, 128), 1)
        for m in range(4):
            part = folded if m == 0 else pltpu.roll(folded, 128 - 32 * m, 1)
            if mask:
                part = jnp.where(lane < 32, part, 0.0)
            tail[16 * m : 16 * m + 16, at, :] = part.astype(BF16).reshape(16, 16, 128)
        return carry

    lax.fori_loop(0, groups, step, 0, unroll=5)


def contract_kernel(n_big, n_small, info_ref, *refs):
    z, half, shift = info_ref[0], info_ref[1], info_ref[2]
    big_refs, refs = refs[:n_big], refs[n_big:]
    small_refs, refs = refs[:n_small], refs[n_small:]
    out_refs, refs = refs[:8], refs[8:]
    sblk, smain, stail, omain, otail = refs[:5]
    pieces = n_small // 4
    for t in range(4):
        spot = lax.rem(t + shift, 4) * 20
        for s in range(pieces):
            ref = small_refs[t * pieces + s]
            n = ref.shape[1]
            for o in range(2):
                sblk[pl.ds(spot + 10 * o + n * s, n)] = ref[o]
    spread_blocks(sblk, smain, stail, 5, True)
    if n_big > 1:
        bblk, bmain, btail = refs[5:]
        for p in range(8):
            spot = lax.rem(z + p, 8) * 20
            for o in range(2):
                sh = half if o == 0 else 1 - half
                piece = big_refs[p][o] if p < 4 else big_refs[4 + o][...] if p == 4 else big_refs[p + 1][o]
                bblk[pl.ds(spot + 10 * sh, 10)] = piece
        spread_blocks(bblk, bmain, btail, 10, False)

    def multiply(rho, carry):
        ends = []
        for m in range(4):
            c = 16 * m + rho
            small = jnp.concatenate([smain[c], stail[c]], axis=1)
            big = big_refs[0][c] if n_big == 1 else jnp.concatenate([bmain[c], btail[c]], axis=1)
            product = lax.dot_general(small, big, NT, preferred_element_type=F32)
            omain[c] = product[:, :128].astype(BF16)
            ends.append(product[:, 128:])
        otail[rho] = jnp.concatenate(ends, axis=1).astype(BF16)
        return carry

    lax.fori_loop(0, 16, multiply, 0, unroll=8)
    for g in range(5):
        at = slice(16 * g, 16 * g + 16)
        main = swap_major(omain[:, at, :])
        tail = swap_major(otail[:, at, :])
        for r in range(16):
            b = 16 * g + r
            out = out_refs[b // 10]
            out[b % 10, :64] = main[r]
            out[b % 10, 64:] = tail[r]


def turn(values):
    return jnp.transpose(values.astype(F32))


def prep_kernel(
    info_ref, x_ref, gain_ref, bias_ref, projw_ref, gatew_ref, ogain_ref, obias_ref, outw_ref,
    gate_ref, field_ref, proj_ref, out0_ref, out1_ref, scales_ref,
):
    half = info_ref[1]

    def local(values):
        return jnp.where(half == 0, values, jnp.concatenate([values[64:], values[:64]], axis=0))

    def column(row):
        return jnp.transpose(jnp.broadcast_to(row, (128, 128)))

    for s in range(4):
        proj_ref[128 * s : 128 * s + 128] = local(turn(projw_ref[1, :, 128 * s : 128 * s + 128])).astype(BF16)
    rolled = local(outw_ref[0].astype(F32))
    out0_ref[...] = jnp.transpose(rolled).astype(BF16)
    out1_ref[...] = local(outw_ref[1].astype(F32)).astype(BF16)
    for n, row in enumerate((ogain_ref[0:1], obias_ref[0:1], ogain_ref[1:2], obias_ref[1:2])):
        scales_ref[n] = local(column(row))
    scales_ref[4] = column(gain_ref[1:2])
    scales_ref[5] = column(bias_ref[1:2])
    gate_w = turn(gatew_ref[0]).astype(BF16)
    eye = lax.broadcasted_iota(jnp.int32, (128, 128), 0) == lax.broadcasted_iota(jnp.int32, (128, 128), 1)
    eye = eye.astype(F32).astype(BF16)
    normed = norm_block(x_ref[...].reshape(1600, 128), gain_ref[0:1], bias_ref[0:1])
    for s in range(x_ref.shape[0]):
        x = x_ref[s]
        rows = widen_rows(normed[160 * s : 160 * s + 160])
        gate_ref[s] = jax.nn.sigmoid(lax.dot_general(gate_w, rows, NT, preferred_element_type=F32))
        field = lax.dot_general(eye, widen_rows(x), NT, preferred_element_type=F32)
        field_ref[s] = field.astype(BF16)


def wide(scale):
    return jnp.concatenate([scale, scale], axis=1)


def middle_kernel(
    own0_ref, own1_ref, own2_ref, other0_ref, other1_ref, other2_ref, gate_ref, field_ref, proj_ref, outw_ref, scales_ref,
    mid_ref, keepl_ref, keepr_ref, sendl_ref, sendr_ref,
):
    lane = lax.broadcasted_iota(jnp.int32, (128, 256), 1)
    for s in range(gate_ref.shape[0]):
        own = own0_ref[s].astype(F32) + own1_ref[s].astype(F32) + own2_ref[s].astype(F32)
        other = other0_ref[s].astype(F32) + other1_ref[s].astype(F32) + other2_ref[s].astype(F32)
        tri = jnp.concatenate([unpack(own), unpack(other)], axis=0)
        upd = norm_chans(tri, wide(scales_ref[0]), wide(scales_ref[1])).astype(BF16)
        turned = jnp.dot(outw_ref[...], upd, preferred_element_type=F32)
        middle = (field_ref[s].astype(F32) + gate_ref[s] * turned).astype(BF16).astype(F32)
        mid_ref[s] = jnp.transpose(middle)[:160].astype(BF16)
        normed = norm_chans(middle, wide(scales_ref[4]), wide(scales_ref[5])).astype(BF16)
        hidden = jnp.dot(proj_ref[...], normed, preferred_element_type=F32)
        for side, (keep_ref, send_ref) in enumerate(((keepl_ref, sendl_ref), (keepr_ref, sendr_ref))):
            h = hidden[256 * side : 256 * side + 256]
            value = jnp.where(lane < 160, jax.nn.sigmoid(h[128:]) * h[:128], 0.0)
            keep_ref[s] = pack(value[:64])
            send_ref[s] = pack(value[64:])


def gate_kernel(x_ref, gain_ref, bias_ref, gatew_ref, gate_ref):
    normed = norm_block(x_ref[...].reshape(1600, 128), gain_ref[1:2], bias_ref[1:2])
    gate = jax.nn.sigmoid(jnp.dot(normed, gatew_ref[1], preferred_element_type=F32))
    gate_ref[...] = gate.reshape(gate_ref.shape)


def last_kernel(
    own0_ref, own1_ref, own2_ref, other0_ref, other1_ref, other2_ref, x_ref, gate_ref, outw_ref, scales_ref, out_ref
):
    for s in range(x_ref.shape[0]):
        own = own0_ref[s].astype(F32) + own1_ref[s].astype(F32) + own2_ref[s].astype(F32)
        other = other0_ref[s].astype(F32) + other1_ref[s].astype(F32) + other2_ref[s].astype(F32)
        tri = jnp.concatenate([unpack(own), unpack(other)], axis=0)
        upd = norm_chans(tri, wide(scales_ref[2]), wide(scales_ref[3]))
        upd = jnp.transpose(upd)[:160].astype(BF16)
        turned = jnp.dot(upd, outw_ref[...], preferred_element_type=F32)
        out_ref[s] = (x_ref[s].astype(F32) + gate_ref[s] * turned).astype(BF16)


def params():
    return pltpu.CompilerParams(vmem_limit_bytes=VMEM_LIMIT)


def cost(flops, nbytes):
    return pl.CostEstimate(flops=flops, bytes_accessed=nbytes, transcendentals=0)


def whole(shape):
    zeros = (0,) * len(shape)
    return pl.BlockSpec(shape, lambda *_: zeros)


def share_call(info, pair, gain, bias, weight):
    return pl.pallas_call(
        share_kernel,
        grid_spec=pltpu.PrefetchScalarGridSpec(
            num_scalar_prefetch=1,
            grid=(2,),
            in_specs=[
                pl.BlockSpec((10, 160, 128), lambda b, info: (2 * info[0] + b, 0, 0)),
                whole((2, 128)), whole((2, 128)), pl.BlockSpec((1, 128, 512), lambda b, info: (0, 0, 0)),
            ],
            out_specs=pl.BlockSpec(
                (None, 10, 80, 128), lambda b, info: (jnp.where(info[1] == 0, b, 1 - b), 0, 0, 0)
            ),
            scratch_shapes=[pltpu.VMEM((128, 128), BF16)],
        ),
        out_shape=jax.ShapeDtypeStruct((2, 10, 80, 128), BF16),
        compiler_params=params(),
        name="share",
    )(info, pair, gain, bias, weight)


def tile_call(info, pair, gain, bias, weight):
    return pl.pallas_call(
        tile_kernel,
        grid_spec=pltpu.PrefetchScalarGridSpec(
            num_scalar_prefetch=1,
            grid=(5,),
            in_specs=[
                pl.BlockSpec((32, 160, 128), lambda b, info: (b, 0, 0)),
                whole((2, 128)), whole((2, 128)), pl.BlockSpec((1, 128, 512), lambda b, info: (0, 0, 0)),
            ],
            out_specs=pl.BlockSpec((64, 32, 256), lambda b, info: (0, b, 0)),
            scratch_shapes=[pltpu.VMEM((128, 128), BF16)],
        ),
        out_shape=jax.ShapeDtypeStruct((64, 160, 256), BF16),
        compiler_params=params(),
        cost_estimate=cost(20 * 10**9, 40 * 2**20),
        name="tile",
    )(info, pair, gain, bias, weight)


def contract_call(info, big, small):
    scratch = [
        pltpu.VMEM((80, 80, 128), BF16),
        pltpu.VMEM((64, 80, 128), BF16), pltpu.VMEM((64, 80, 128), BF16),
        pltpu.VMEM((64, 80, 128), BF16), pltpu.VMEM((16, 80, 128), BF16),
    ]
    if len(big) > 1:
        scratch += [
            pltpu.VMEM((160, 80, 128), BF16),
            pltpu.VMEM((64, 160, 128), BF16), pltpu.VMEM((64, 160, 128), BF16),
        ]
    args = list(big) + list(small)
    return pl.pallas_call(
        functools.partial(contract_kernel, len(big), len(small)),
        in_specs=[pl.BlockSpec(memory_space=pltpu.SMEM)] + [pl.BlockSpec(memory_space=pltpu.VMEM)] * len(args),
        out_specs=[pl.BlockSpec(memory_space=pltpu.VMEM)] * 8,
        out_shape=[jax.ShapeDtypeStruct((10, 80, 128), BF16)] * 8,
        scratch_shapes=scratch,
        compiler_params=params(),
        cost_estimate=cost(30 * 10**9, 60 * 2**20),
        name="contract",
    )(info, *args)


def simple_call(kernel, name, shapes, args, smem=0, flops=10**9):
    vmem = pl.BlockSpec(memory_space=pltpu.VMEM)
    return pl.pallas_call(
        kernel,
        in_specs=[pl.BlockSpec(memory_space=pltpu.SMEM)] * smem + [vmem] * (len(args) - smem),
        out_specs=[vmem] * len(shapes),
        out_shape=[jax.ShapeDtypeStruct(*s) for s in shapes],
        compiler_params=params(),
        cost_estimate=cost(flops, 8 * 2**20),
        name=name,
    )(*args)


def shift_by(values, axis, step):
    n = lax.axis_size(axis)
    return lax.ppermute(values, axis, [(i, (i + step) % n) for i in range(n)])


def swap_cores(values):
    return lax.ppermute(values, "depth", [(d, d ^ 1) for d in range(lax.axis_size("depth"))])


def gather4(values, axis):
    return [values, shift_by(values, axis, -1), shift_by(values, axis, 2), shift_by(values, axis, 1)]


def add2(a, b):
    return (a.astype(F32) + b.astype(F32)).astype(BF16)


def cross_by(values, axis, step):
    n, depth = lax.axis_size(axis), lax.axis_size("depth")
    pairs = [(i * depth + d, (i + step) % n * depth + (d ^ 1)) for i in range(n) for d in range(depth)]
    return lax.ppermute(values, (axis, "depth"), pairs)


def scatter4(parts, axis):
    p0, p1, p2, p3 = (parts[2 * u : 2 * u + 2] for u in range(4))
    up2 = shift_by(p2[0], axis, 1)
    down2 = shift_by(p2[1], axis, -1)
    up1 = cross_by(p1[1], axis, 1)
    down1 = shift_by(p3[0], axis, -1)
    up0 = shift_by(add2(p1[0], up2), axis, 1)
    down0 = cross_by(add2(p3[1], down2), axis, -1)
    return p0[0], up0, down1, swap_cores(p0[1]), up1, down0


def ring8(x, axis=0, beside=()):
    got = [x] + [None] * 7
    for k in range(1, 4):
        if k == 3 and beside:
            got[6], got[2], *beside = lax.optimization_barrier((got[6], got[2], *beside))
        got[8 - k] = shift_by(got[(9 - k) % 8], "depth", 2)
        got[k] = shift_by(got[k - 1], "depth", -2)
    first, second = jnp.split(got[5], 2, axis)[0], jnp.split(got[3], 2, axis)[1]
    got[4] = [shift_by(first, "depth", 2), shift_by(second, "depth", -2)]
    return got, beside


def assemble_kernel(first, steps, info_ref, *refs):
    out_ref, sem = refs[-2], refs[-1]
    pieces = refs[: 2 * len(steps)] if first else refs[1:-2]
    z, half = info_ref[0], info_ref[1]
    copies = []
    for n, ref in enumerate(pieces):
        p, side = steps[n // 2], n % 2
        core = half if side == 0 else 1 - half
        row = lax.rem(z + p, 8) * 20 + 10 * core
        copies.append(pltpu.make_async_copy(ref, out_ref.at[pl.ds(row, 10)], sem.at[n]))
    for copy in copies:
        copy.start()
    for copy in copies:
        copy.wait()


def assemble_call(info, steps, pieces, base=None):
    anywhere = pl.BlockSpec(memory_space=pl.ANY)
    args = [info] + ([] if base is None else [base]) + list(pieces)
    return pl.pallas_call(
        functools.partial(assemble_kernel, base is None, steps),
        in_specs=(
            [pl.BlockSpec(memory_space=pltpu.SMEM)]
            + [anywhere] * (base is not None)
            + [pl.BlockSpec(memory_space=pltpu.VMEM)] * len(pieces)
        ),
        out_specs=anywhere,
        out_shape=jax.ShapeDtypeStruct((160, 160, 128), BF16),
        scratch_shapes=[pltpu.SemaphoreType.DMA((len(pieces),))],
        input_output_aliases={} if base is None else {1: 0},
        compiler_params=params(),
        name="assemble",
    )(*args)


def on_device(pair, in_gain, in_bias, proj_weight, gate_weight, out_gain, out_bias, out_weight):
    layer = lax.axis_index("depth")
    z, half = layer // 2, layer % 2
    here, there = lax.axis_index("row"), lax.axis_index("col")
    info = jnp.stack([z, half, (here - there + 4) % 4]).astype(jnp.int32)
    info1 = jnp.stack([z, half, (there - here + 4) % 4]).astype(jnp.int32)

    same_core = [list(range(c, 16, 2)) for c in range(2)]

    right = share_call(info, pair, in_gain, in_bias, proj_weight)
    right_all = gather4(right, "row")
    left = tile_call(info, pair, in_gain, in_bias, proj_weight)
    columns = lax.dynamic_slice_in_dim(pair, 10 * layer, 10, 1).transpose(1, 0, 2)
    gate, field, proj, out0, out1, scales = simple_call(
        prep_kernel, "prep",
        [((10, 128, 256), F32), ((10, 128, 256), BF16), ((512, 128), BF16), ((128, 128), BF16),
         ((128, 128), BF16), ((6, 128, 128), F32)],
        [info, columns, in_gain, in_bias, proj_weight, gate_weight, out_gain, out_bias, out_weight],
        smem=1,
    )
    right_all[3], gate = lax.optimization_barrier((right_all[3], gate))
    addends = scatter4(contract_call(info, [left], right_all), "col")

    packed = ((10, 80, 128), BF16)
    middle, keep_l, keep_r, send_l, send_r = simple_call(
        middle_kernel, "middle", [((10, 160, 128), BF16)] + [packed] * 4,
        [*addends, gate, field, proj, out0, scales],
    )
    rights = jnp.stack([keep_r, swap_cores(send_r)])
    lefts = gather4(jnp.stack([keep_l, swap_cores(send_l)]), "col")
    rights, _ = ring8(rights)
    big = rights[:4] + [v[0] for v in rights[4]] + rights[5:]
    parts = contract_call(info1, big, lefts)
    addends = scatter4(parts, "row")
    moved = lax.all_to_all(
        middle.reshape(10, 8, 20, 128), "depth", 1, 0, axis_index_groups=same_core, tiled=False
    )
    own_rows = lax.dynamic_slice_in_dim(moved, 10 * half, 10, 2)
    got_rows = swap_cores(lax.dynamic_slice_in_dim(moved, 10 * (1 - half), 10, 2))
    first, second = jnp.where(half == 0, own_rows, got_rows), jnp.where(half == 0, got_rows, own_rows)
    rows = jnp.stack([first, second], axis=1).reshape(160, 10, 128).transpose(1, 0, 2)
    (gate,) = simple_call(
        gate_kernel, "gate", [((10, 160, 128), F32)], [rows, in_gain, in_bias, gate_weight]
    )
    (result,) = simple_call(
        last_kernel, "last", [((10, 160, 128), BF16)], [*addends, rows, gate, out1, scales]
    )
    got, _ = ring8(result)
    got[4] = jnp.concatenate(got[4], axis=0)
    final = jnp.zeros(pair.shape, BF16)
    for p in (0, 1, 7, 2, 6, 3, 5, 4):
        place = (z + p) % 8 * 20
        final = lax.dynamic_update_slice(final, got[p], (place + 10 * half, 0, 0))
        final = lax.dynamic_update_slice(final, swap_cores(got[p]), (place + 10 * (1 - half), 0, 0))
    return final


def solution(mesh):
    placed = (P("row", "col", None), P(), P(), P(), P(), P(), P(), P())
    return jax.shard_map(
        on_device, mesh=mesh, in_specs=placed, out_specs=P("row", "col", None), check_vma=False
    )
```

```python
import functools

import jax
import jax.numpy as jnp
from jax import lax
from jax.experimental import pallas as pl
from jax.experimental.pallas import tpu as pltpu
from jax.sharding import PartitionSpec as P

F32 = jnp.float32
BF16 = jnp.bfloat16
VMEM_LIMIT = 60 * 1024 * 1024
NT = (((1,), (1,)), ((), ()))


def norm_block(rows, gain, bias):
    ones = jnp.full((128, 128), 1 / 128, BF16)
    centred = rows.astype(F32) - jnp.dot(rows, ones, preferred_element_type=F32)
    spread = jnp.dot((centred * centred).astype(BF16), ones, preferred_element_type=F32)
    return (centred * lax.rsqrt(spread + 1e-05) * gain + bias).astype(BF16)


def norm_chans(values, gain, bias):
    mean = jnp.mean(values, axis=0, keepdims=True)
    centred = values - mean
    spread = jnp.mean(centred * centred, axis=0, keepdims=True)
    return centred * lax.rsqrt(spread + 1e-05) * gain + bias


def widen_rows(rows):
    return jnp.concatenate([rows, jnp.zeros((256 - rows.shape[0], rows.shape[1]), rows.dtype)], axis=0)


def fold(tail):
    total = tail[:16]
    for m in range(1, 4):
        total = total + pltpu.roll(tail[16 * m : 16 * m + 16], 32 * m, 1)
    return total


def unfold(packed):
    parts = [packed] + [pltpu.roll(packed, 128 - 32 * m, 1) for m in range(1, 4)]
    tail = jnp.concatenate(parts, axis=0)
    lane = lax.broadcasted_iota(jnp.int32, tail.shape, 1)
    return jnp.where(lane < 32, tail, 0.0)


def pack(chans):
    return jnp.concatenate([chans[:, :128], fold(chans[:, 128:])], axis=0).astype(BF16)


def unpack(block):
    wide = block.astype(F32)
    return jnp.concatenate([wide[:64], unfold(wide[64:])], axis=1)


def gated_chans(weight_t, normed):
    hidden = lax.dot_general(weight_t, normed, NT, preferred_element_type=F32)
    n = weight_t.shape[0] // 2
    return jax.nn.sigmoid(hidden[n:]) * hidden[:n]


def swap_major(values):
    return jnp.swapaxes(values, 0, 1)


def pick_weight(weight_ref, half, first):
    both = []
    for start in (first, first + 128):
        pane = weight_ref[0, :, start : start + 128].astype(F32)
        both.append(jnp.where(half == 0, pane[:, :64], pane[:, 64:]))
    return jnp.transpose(jnp.concatenate(both, axis=1)).astype(BF16)


def share_kernel(info_ref, x_ref, gain_ref, bias_ref, weight_ref, out_ref, weight):
    @pl.when(pl.program_id(0) == 0)
    def _():
        weight[...] = pick_weight(weight_ref, info_ref[1], 256)

    per = x_ref.shape[0]
    normed = norm_block(x_ref[...].reshape(per * 160, 128), gain_ref[0:1], bias_ref[0:1])
    for r in range(per):
        out_ref[r] = pack(gated_chans(weight[...], widen_rows(normed[160 * r : 160 * r + 160])))


def tile_kernel(info_ref, x_ref, gain_ref, bias_ref, weight_ref, out_ref, weight):
    @pl.when(pl.program_id(0) == 0)
    def _():
        weight[...] = pick_weight(weight_ref, info_ref[1], 0)

    per = x_ref.shape[0]
    normed = norm_block(x_ref[...].reshape(per * 160, 128), gain_ref[0:1], bias_ref[0:1])
    rows = []
    for r in range(per):
        values = gated_chans(weight[...], normed[160 * r : 160 * r + 160]).astype(BF16)
        rows.append(jnp.concatenate([values, jnp.zeros((64, 96), BF16)], axis=1))
    for side in range(2):
        at = slice(128 * side, 128 * side + 128)
        out_ref[:, :, at] = swap_major(jnp.stack([row[:, at] for row in rows]))


def spread_blocks(blocks, main, tail, groups, mask):
    def step(g, carry):
        at = pl.ds(pl.multiple_of(g * 16, 16), 16)
        x = blocks[at]
        main[:, at, :] = swap_major(x[:, :64])
        folded = swap_major(x[:, 64:]).astype(F32).reshape(256, 128)
        lane = lax.broadcasted_iota(jnp.int32, (256, 128), 1)
        for m in range(4):
            part = folded if m == 0 else pltpu.roll(folded, 128 - 32 * m, 1)
            if mask:
                part = jnp.where(lane < 32, part, 0.0)
            tail[16 * m : 16 * m + 16, at, :] = part.astype(BF16).reshape(16, 16, 128)
        return carry

    lax.fori_loop(0, groups, step, 0, unroll=5)


def contract_kernel(n_big, n_small, info_ref, *refs):
    z, half, shift = info_ref[0], info_ref[1], info_ref[2]
    big_refs, refs = refs[:n_big], refs[n_big:]
    small_refs, refs = refs[:n_small], refs[n_small:]
    out_refs, refs = refs[:8], refs[8:]
    sblk, smain, stail, omain, otail = refs[:5]
    pieces = n_small // 4
    for t in range(4):
        spot = lax.rem(t + shift, 4) * 20
        for s in range(pieces):
            ref = small_refs[t * pieces + s]
            n = ref.shape[1]
            for o in range(2):
                sblk[pl.ds(spot + 10 * o + n * s, n)] = ref[o]
    spread_blocks(sblk, smain, stail, 5, True)
    if n_big > 1:
        bblk, bmain, btail = refs[5:]
        for p in range(8):
            spot = lax.rem(z + p, 8) * 20
            for o in range(2):
                sh = half if o == 0 else 1 - half
                piece = big_refs[p][o] if p < 4 else big_refs[4 + o][...] if p == 4 else big_refs[p + 1][o]
                bblk[pl.ds(spot + 10 * sh, 10)] = piece
        spread_blocks(bblk, bmain, btail, 10, False)

    def multiply(rho, carry):
        ends = []
        for m in range(4):
            c = 16 * m + rho
            small = jnp.concatenate([smain[c], stail[c]], axis=1)
            big = big_refs[0][c] if n_big == 1 else jnp.concatenate([bmain[c], btail[c]], axis=1)
            product = lax.dot_general(small, big, NT, preferred_element_type=F32)
            omain[c] = product[:, :128].astype(BF16)
            ends.append(product[:, 128:])
        otail[rho] = jnp.concatenate(ends, axis=1).astype(BF16)
        return carry

    lax.fori_loop(0, 16, multiply, 0, unroll=16)
    for g in range(5):
        at = slice(16 * g, 16 * g + 16)
        main = swap_major(omain[:, at, :])
        tail = swap_major(otail[:, at, :])
        for r in range(16):
            b = 16 * g + r
            out = out_refs[b // 10]
            out[b % 10, :64] = main[r]
            out[b % 10, 64:] = tail[r]


def turn(values):
    return jnp.transpose(values.astype(F32))


def prep_kernel(
    info_ref, x_ref, gain_ref, bias_ref, projw_ref, gatew_ref, ogain_ref, obias_ref, outw_ref,
    gate_ref, field_ref, proj_ref, out0_ref, out1_ref, scales_ref,
):
    half = info_ref[1]

    def local(values):
        return jnp.where(half == 0, values, jnp.concatenate([values[64:], values[:64]], axis=0))

    def column(row):
        return jnp.transpose(jnp.broadcast_to(row, (128, 128)))

    for s in range(4):
        proj_ref[128 * s : 128 * s + 128] = local(turn(projw_ref[1, :, 128 * s : 128 * s + 128])).astype(BF16)
    rolled = local(outw_ref[0].astype(F32))
    out0_ref[...] = jnp.transpose(rolled).astype(BF16)
    out1_ref[...] = local(outw_ref[1].astype(F32)).astype(BF16)
    for n, row in enumerate((ogain_ref[0:1], obias_ref[0:1], ogain_ref[1:2], obias_ref[1:2])):
        scales_ref[n] = local(column(row))
    scales_ref[4] = column(gain_ref[1:2])
    scales_ref[5] = column(bias_ref[1:2])
    gate_w = turn(gatew_ref[0]).astype(BF16)
    eye = lax.broadcasted_iota(jnp.int32, (128, 128), 0) == lax.broadcasted_iota(jnp.int32, (128, 128), 1)
    eye = eye.astype(F32).astype(BF16)
    normed = norm_block(x_ref[...].reshape(1600, 128), gain_ref[0:1], bias_ref[0:1])
    for s in range(x_ref.shape[0]):
        x = x_ref[s]
        rows = widen_rows(normed[160 * s : 160 * s + 160])
        gate_ref[s] = jax.nn.sigmoid(lax.dot_general(gate_w, rows, NT, preferred_element_type=F32))
        field = lax.dot_general(eye, widen_rows(x), NT, preferred_element_type=F32)
        field_ref[s] = field.astype(BF16)


def wide(scale):
    return jnp.concatenate([scale, scale], axis=1)


def middle_kernel(
    own0_ref, own1_ref, own2_ref, other0_ref, other1_ref, other2_ref, gate_ref, field_ref, proj_ref, outw_ref, scales_ref,
    mid_ref, keepl_ref, keepr_ref, sendl_ref, sendr_ref,
):
    lane = lax.broadcasted_iota(jnp.int32, (128, 256), 1)
    for s in range(gate_ref.shape[0]):
        own = own0_ref[s].astype(F32) + own1_ref[s].astype(F32) + own2_ref[s].astype(F32)
        other = other0_ref[s].astype(F32) + other1_ref[s].astype(F32) + other2_ref[s].astype(F32)
        tri = jnp.concatenate([unpack(own), unpack(other)], axis=0)
        upd = norm_chans(tri, wide(scales_ref[0]), wide(scales_ref[1])).astype(BF16)
        turned = jnp.dot(outw_ref[...], upd, preferred_element_type=F32)
        middle = (field_ref[s].astype(F32) + gate_ref[s] * turned).astype(BF16).astype(F32)
        turned_middle = jnp.transpose(middle)
        for d in range(8):
            mid_ref[s, d] = turned_middle[20 * d : 20 * d + 20].astype(BF16)
        normed = norm_chans(middle, wide(scales_ref[4]), wide(scales_ref[5])).astype(BF16)
        hidden = jnp.dot(proj_ref[...], normed, preferred_element_type=F32)
        for side, (keep_ref, send_ref) in enumerate(((keepl_ref, sendl_ref), (keepr_ref, sendr_ref))):
            h = hidden[256 * side : 256 * side + 256]
            value = jnp.where(lane < 160, jax.nn.sigmoid(h[128:]) * h[:128], 0.0)
            keep_ref[s] = pack(value[:64])
            send_ref[s] = pack(value[64:])


def gate_kernel(x_ref, gain_ref, bias_ref, gatew_ref, gate_ref):
    normed = norm_block(x_ref[...].reshape(1600, 128), gain_ref[1:2], bias_ref[1:2])
    gate = jax.nn.sigmoid(jnp.dot(normed, gatew_ref[1], preferred_element_type=F32))
    gate_ref[...] = gate.reshape(gate_ref.shape)


def last_kernel(
    own0_ref, own1_ref, own2_ref, other0_ref, other1_ref, other2_ref, x_ref, gate_ref, outw_ref, scales_ref, out_ref
):
    for s in range(x_ref.shape[0]):
        own = own0_ref[s].astype(F32) + own1_ref[s].astype(F32) + own2_ref[s].astype(F32)
        other = other0_ref[s].astype(F32) + other1_ref[s].astype(F32) + other2_ref[s].astype(F32)
        tri = jnp.concatenate([unpack(own), unpack(other)], axis=0)
        upd = norm_chans(tri, wide(scales_ref[2]), wide(scales_ref[3]))
        upd = jnp.transpose(upd)[:160].astype(BF16)
        turned = jnp.dot(upd, outw_ref[...], preferred_element_type=F32)
        out_ref[s] = (x_ref[s].astype(F32) + gate_ref[s] * turned).astype(BF16)


def params():
    return pltpu.CompilerParams(vmem_limit_bytes=VMEM_LIMIT)


def cost(flops, nbytes):
    return pl.CostEstimate(flops=flops, bytes_accessed=nbytes, transcendentals=0)


def whole(shape):
    zeros = (0,) * len(shape)
    return pl.BlockSpec(shape, lambda *_: zeros)


def share_call(info, pair, gain, bias, weight):
    return pl.pallas_call(
        share_kernel,
        grid_spec=pltpu.PrefetchScalarGridSpec(
            num_scalar_prefetch=1,
            grid=(2,),
            in_specs=[
                pl.BlockSpec((10, 160, 128), lambda b, info: (2 * info[0] + b, 0, 0)),
                whole((2, 128)), whole((2, 128)), pl.BlockSpec((1, 128, 512), lambda b, info: (0, 0, 0)),
            ],
            out_specs=pl.BlockSpec(
                (None, 10, 80, 128), lambda b, info: (jnp.where(info[1] == 0, b, 1 - b), 0, 0, 0)
            ),
            scratch_shapes=[pltpu.VMEM((128, 128), BF16)],
        ),
        out_shape=jax.ShapeDtypeStruct((2, 10, 80, 128), BF16),
        compiler_params=params(),
        name="share",
    )(info, pair, gain, bias, weight)


def tile_call(info, pair, gain, bias, weight):
    return pl.pallas_call(
        tile_kernel,
        grid_spec=pltpu.PrefetchScalarGridSpec(
            num_scalar_prefetch=1,
            grid=(5,),
            in_specs=[
                pl.BlockSpec((32, 160, 128), lambda b, info: (b, 0, 0)),
                whole((2, 128)), whole((2, 128)), pl.BlockSpec((1, 128, 512), lambda b, info: (0, 0, 0)),
            ],
            out_specs=pl.BlockSpec((64, 32, 256), lambda b, info: (0, b, 0)),
            scratch_shapes=[pltpu.VMEM((128, 128), BF16)],
        ),
        out_shape=jax.ShapeDtypeStruct((64, 160, 256), BF16),
        compiler_params=params(),
        cost_estimate=cost(20 * 10**9, 40 * 2**20),
        name="tile",
    )(info, pair, gain, bias, weight)


def contract_call(info, big, small):
    scratch = [
        pltpu.VMEM((80, 80, 128), BF16),
        pltpu.VMEM((64, 80, 128), BF16), pltpu.VMEM((64, 80, 128), BF16),
        pltpu.VMEM((64, 80, 128), BF16), pltpu.VMEM((16, 80, 128), BF16),
    ]
    if len(big) > 1:
        scratch += [
            pltpu.VMEM((160, 80, 128), BF16),
            pltpu.VMEM((64, 160, 128), BF16), pltpu.VMEM((64, 160, 128), BF16),
        ]
    args = list(big) + list(small)
    return pl.pallas_call(
        functools.partial(contract_kernel, len(big), len(small)),
        in_specs=[pl.BlockSpec(memory_space=pltpu.SMEM)] + [pl.BlockSpec(memory_space=pltpu.VMEM)] * len(args),
        out_specs=[pl.BlockSpec(memory_space=pltpu.VMEM)] * 8,
        out_shape=[jax.ShapeDtypeStruct((10, 80, 128), BF16)] * 8,
        scratch_shapes=scratch,
        compiler_params=params(),
        cost_estimate=cost(30 * 10**9, 60 * 2**20),
        name="contract",
    )(info, *args)


def simple_call(kernel, name, shapes, args, smem=0, flops=10**9):
    vmem = pl.BlockSpec(memory_space=pltpu.VMEM)
    return pl.pallas_call(
        kernel,
        in_specs=[pl.BlockSpec(memory_space=pltpu.SMEM)] * smem + [vmem] * (len(args) - smem),
        out_specs=[vmem] * len(shapes),
        out_shape=[jax.ShapeDtypeStruct(*s) for s in shapes],
        compiler_params=params(),
        cost_estimate=cost(flops, 8 * 2**20),
        name=name,
    )(*args)


def shift_by(values, axis, step):
    n = lax.axis_size(axis)
    return lax.ppermute(values, axis, [(i, (i + step) % n) for i in range(n)])


def swap_cores(values):
    return lax.ppermute(values, "depth", [(d, d ^ 1) for d in range(lax.axis_size("depth"))])


def gather4(values, axis):
    return [values, shift_by(values, axis, -1), shift_by(values, axis, 2), shift_by(values, axis, 1)]


def add2(a, b):
    return (a.astype(F32) + b.astype(F32)).astype(BF16)


def cross_by(values, axis, step):
    n, depth = lax.axis_size(axis), lax.axis_size("depth")
    pairs = [(i * depth + d, (i + step) % n * depth + (d ^ 1)) for i in range(n) for d in range(depth)]
    return lax.ppermute(values, (axis, "depth"), pairs)


def scatter4(parts, axis):
    p0, p1, p2, p3 = (parts[2 * u : 2 * u + 2] for u in range(4))
    up2 = shift_by(p2[0], axis, 1)
    down2 = shift_by(p2[1], axis, -1)
    up1 = cross_by(p1[1], axis, 1)
    down1 = shift_by(p3[0], axis, -1)
    up0 = shift_by(add2(p1[0], up2), axis, 1)
    down0 = cross_by(add2(p3[1], down2), axis, -1)
    return p0[0], up0, down1, swap_cores(p0[1]), up1, down0


def ring8(x, axis=0, beside=()):
    got = [x] + [None] * 7
    for k in range(1, 4):
        if k == 3 and beside:
            got[6], got[2], *beside = lax.optimization_barrier((got[6], got[2], *beside))
        got[8 - k] = shift_by(got[(9 - k) % 8], "depth", 2)
        got[k] = shift_by(got[k - 1], "depth", -2)
    first, second = jnp.split(got[5], 2, axis)[0], jnp.split(got[3], 2, axis)[1]
    got[4] = [shift_by(first, "depth", 2), shift_by(second, "depth", -2)]
    return got, beside


def assemble_kernel(first, steps, info_ref, *refs):
    out_ref, sem = refs[-2], refs[-1]
    pieces = refs[: 2 * len(steps)] if first else refs[1:-2]
    z, half = info_ref[0], info_ref[1]
    copies = []
    for n, ref in enumerate(pieces):
        p, side = steps[n // 2], n % 2
        core = half if side == 0 else 1 - half
        row = lax.rem(z + p, 8) * 20 + 10 * core
        copies.append(pltpu.make_async_copy(ref, out_ref.at[pl.ds(row, 10)], sem.at[n]))
    for copy in copies:
        copy.start()
    for copy in copies:
        copy.wait()


def assemble_call(info, steps, pieces, base=None):
    anywhere = pl.BlockSpec(memory_space=pl.ANY)
    args = [info] + ([] if base is None else [base]) + list(pieces)
    return pl.pallas_call(
        functools.partial(assemble_kernel, base is None, steps),
        in_specs=(
            [pl.BlockSpec(memory_space=pltpu.SMEM)]
            + [anywhere] * (base is not None)
            + [pl.BlockSpec(memory_space=pltpu.VMEM)] * len(pieces)
        ),
        out_specs=anywhere,
        out_shape=jax.ShapeDtypeStruct((160, 160, 128), BF16),
        scratch_shapes=[pltpu.SemaphoreType.DMA((len(pieces),))],
        input_output_aliases={} if base is None else {1: 0},
        compiler_params=params(),
        name="assemble",
    )(*args)


def on_device(pair, in_gain, in_bias, proj_weight, gate_weight, out_gain, out_bias, out_weight):
    layer = lax.axis_index("depth")
    z, half = layer // 2, layer % 2
    here, there = lax.axis_index("row"), lax.axis_index("col")
    info = jnp.stack([z, half, (here - there + 4) % 4]).astype(jnp.int32)
    info1 = jnp.stack([z, half, (there - here + 4) % 4]).astype(jnp.int32)

    same_core = [list(range(c, 16, 2)) for c in range(2)]

    right = share_call(info, pair, in_gain, in_bias, proj_weight)
    right_all = gather4(right, "row")
    left = tile_call(info, pair, in_gain, in_bias, proj_weight)
    columns = lax.dynamic_slice_in_dim(pair, 10 * layer, 10, 1).transpose(1, 0, 2)
    gate, field, proj, out0, out1, scales = simple_call(
        prep_kernel, "prep",
        [((10, 128, 256), F32), ((10, 128, 256), BF16), ((512, 128), BF16), ((128, 128), BF16),
         ((128, 128), BF16), ((6, 128, 128), F32)],
        [info, columns, in_gain, in_bias, proj_weight, gate_weight, out_gain, out_bias, out_weight],
        smem=1,
    )
    right_all[3], gate = lax.optimization_barrier((right_all[3], gate))
    addends = scatter4(contract_call(info, [left], right_all), "col")

    packed = ((10, 80, 128), BF16)
    middle, keep_l, keep_r, send_l, send_r = simple_call(
        middle_kernel, "middle", [((10, 8, 20, 128), BF16)] + [packed] * 4,
        [*addends, gate, field, proj, out0, scales],
    )
    rights = jnp.stack([keep_r, swap_cores(send_r)])
    lefts = gather4(jnp.stack([keep_l, swap_cores(send_l)]), "col")
    rights, _ = ring8(rights)
    big = rights[:4] + [v[0] for v in rights[4]] + rights[5:]
    parts = contract_call(info1, big, lefts)
    addends = scatter4(parts, "row")
    moved = lax.all_to_all(
        middle, "depth", 1, 0, axis_index_groups=same_core, tiled=False
    )
    own_rows = lax.dynamic_slice_in_dim(moved, 10 * half, 10, 2)
    got_rows = swap_cores(lax.dynamic_slice_in_dim(moved, 10 * (1 - half), 10, 2))
    first, second = jnp.where(half == 0, own_rows, got_rows), jnp.where(half == 0, got_rows, own_rows)
    rows = jnp.stack([first, second], axis=1).reshape(160, 10, 128).transpose(1, 0, 2)
    (gate,) = simple_call(
        gate_kernel, "gate", [((10, 160, 128), F32)], [rows, in_gain, in_bias, gate_weight]
    )
    (result,) = simple_call(
        last_kernel, "last", [((10, 160, 128), BF16)], [*addends, rows, gate, out1, scales]
    )
    got, _ = ring8(result)
    got[4] = jnp.concatenate(got[4], axis=0)
    final = jnp.zeros(pair.shape, BF16)
    for p in (0, 1, 7, 2, 6, 3, 5, 4):
        place = (z + p) % 8 * 20
        final = lax.dynamic_update_slice(final, got[p], (place + 10 * half, 0, 0))
        final = lax.dynamic_update_slice(final, swap_cores(got[p]), (place + 10 * (1 - half), 0, 0))
    return final


def solution(mesh):
    placed = (P("row", "col", None), P(), P(), P(), P(), P(), P(), P())
    return jax.shard_map(
        on_device, mesh=mesh, in_specs=placed, out_specs=P("row", "col", None), check_vma=False
    )
```
